256 devices in a mesh: ctx: 64 (over y, z, x_lo), head: 4 (over x_hi, core).
Axes of the slice: x: 4 (x_hi: 2, x_lo: 2; x = x_hi * 2 + x_lo), y: 4, z: 8, core: 2. Of those that a mesh axis runs over, the one named last changes fastest.
Arguments:
- queries: bfloat16 [32, 8192, 128], P('head', 'ctx'), as said below
- keys: bfloat16 [4, 8192, 128], P('head', 'ctx'), as said below
- values: bfloat16 [4, 8192, 128], P('head', 'ctx'), may hold values from -6 to 6
- evict_logits: float32 [4, 8192], P('head', 'ctx'), may hold values from -12 to 12
- block_order: int32 [64, 2], replicated, may hold values from 0 to 127, as said below
- grad_y: bfloat16 [8192, 5120], P(('ctx', 'head')), may hold values from -24 to 24
- w_out: bfloat16 [4096, 5120], P('head'), may hold values from -0.09375 to 0.09375
Outputs:
- query_grad: bfloat16 [32, 8192, 128], P('head', 'ctx')
- key_grad: float32 [4, 8192, 128], P('head', 'ctx')
- value_grad: float32 [4, 8192, 128], P('head', 'ctx')
- logit_grad: float32 [4, 8192], P('head', 'ctx')
The draws below stay inside these ranges and needn't reach their ends.
Inputs may be any that keep to these rules, and one draw needn't show every extreme that they name: `block_order`: row s holds the two position blocks of ctx shard s: a block c below 64 in column 0 and the block 127 - c in column 1; every block appears once. `queries`: real values of order one or more. `keys`: real values of order one or more.
All inputs are finite; a program needn't handle non-finite values.
Results may differ from the reference program's by a relative error of at most 0.04.
Values may be sent and summed in bfloat16 or wider, within the bound.
No kernel may reach another device: no remote copies, remote signals or barrier semaphores. Data moves between devices by JAX's collectives and lax.ppermute only.
A program may use at most 64 MiB of HBM per device.

```python
import math
import jax
import jax.numpy as jnp
from jax import lax

D = 5120
QH = 32
KVH = 4
HD = 128
WINDOW = 256
TOK_DEV = 128
GROUP = 8
HALF = 64
TOKENS = 8192
BLOCKS = 128


def draw_queries(key, part):
    key = jax.random.fold_in(key, 3)
    drawn = jax.random.normal(key, (QH, TOKENS, HD), jnp.float32)
    return drawn.astype(jnp.bfloat16)


def draw_keys(key, part):
    key = jax.random.fold_in(key, 5)
    drawn = jax.random.normal(key, (KVH, TOKENS, HD), jnp.float32)
    return drawn.astype(jnp.bfloat16)


def draw_block_order(key, part):
    key = jax.random.fold_in(key, 7)
    ordering = jax.random.permutation(key, BLOCKS // 2).astype(jnp.int32)
    return jnp.stack([ordering, BLOCKS - 1 - ordering], axis=1).astype(jnp.int32)


def steps_of(own_key, extent, cuts, smallest, largest):
    level, own = 1.0, jax.random.fold_in(own_key, 6)
    for dim, shards_of in cuts:
        steps = jnp.exp(jax.random.uniform(jax.random.fold_in(own, dim), (shards_of,), jnp.float32, smallest / len(cuts), largest / len(cuts)))
        level = level * jnp.repeat(steps, extent[dim] // shards_of).reshape([-1 if axis == dim else 1 for axis in range(len(extent))])
    return level


def scatter_about(own_key, extent, spread, most, pieces=(), kind=jnp.bfloat16):
    values = spread * jax.random.normal(own_key, extent, jnp.float32)
    if pieces:
        values = values * steps_of(own_key, extent, pieces, -0.22, 0.18)
    return jnp.clip(values, -most, most).astype(kind)


def setup_inputs(seed: int = 0) -> dict:
    splits = jax.random.split(jax.random.key(seed), 8)
    return {
        "queries": draw_queries(jax.random.fold_in(splits[7], 71), 0),
        "keys": draw_keys(jax.random.fold_in(splits[7], 71), 0),
        "values": scatter_about(splits[2], (KVH, TOKENS, HD), 1.0, 6.0, ((0, 4), (1, 64))),
        "evict_logits": scatter_about(splits[3], (KVH, TOKENS), 3.0, 12.0, ((0, 4), (1, 64)), jnp.float32),
        "block_order": draw_block_order(jax.random.fold_in(splits[7], 71), 0),
        "grad_y": scatter_about(splits[5], (TOKENS, D), 4.0, 24.0, ((0, 256),)),
        "w_out": scatter_about(splits[6], (QH * HD, D), (QH * HD) ** -0.5, 0.09375, ((0, 4),)),
    }


def token_positions(block_order):
    token_index = jnp.arange(TOKENS, dtype=jnp.int32)
    owner_shard = token_index // TOK_DEV
    inside = token_index % TOK_DEV
    return block_order[owner_shard, inside // HALF] * HALF + inside % HALF

def reference(queries, keys, values, evict_logits, block_order, grad_y, w_out):
    position = token_positions(block_order)
    scaling = 1.0 / math.sqrt(HD)
    cotangent = jnp.dot(grad_y, w_out.T, preferred_element_type=jnp.float32).astype(jnp.bfloat16)
    cotangent = cotangent.reshape(TOKENS, QH, HD).transpose(1, 0, 2)
    distance = position[:, None] - position[None, :]
    visible = distance >= 0
    delayed = distance >= WINDOW

    def per_head(head_index):
        shared_head = head_index // GROUP
        query_head = queries[head_index]
        key_head = keys[shared_head]
        value_head = values[shared_head]
        cotangent_head = cotangent[head_index]
        scores = jnp.dot(query_head, key_head.T, preferred_element_type=jnp.float32) * scaling
        scores = scores - jnp.where(delayed, jax.nn.softplus(evict_logits[shared_head])[None, :], 0.0)
        scores = jnp.where(visible, scores, -jnp.inf)
        row_peak = lax.optimization_barrier(jnp.max(scores, axis=1, keepdims=True))
        log_norm = row_peak + jnp.log(lax.optimization_barrier(jnp.sum(jnp.exp(scores - row_peak), axis=1, keepdims=True)))
        probs = jnp.where(visible, jnp.exp(scores - log_norm), 0.0)
        prob_grad = jnp.dot(cotangent_head, value_head.T, preferred_element_type=jnp.float32)
        mean_grad = lax.optimization_barrier(jnp.sum(probs * prob_grad, axis=1, keepdims=True))
        score_grad = probs * (prob_grad - mean_grad)
        grad_half = score_grad.astype(jnp.bfloat16)
        probs_half = probs.astype(jnp.bfloat16)
        head_query_grad = (jnp.dot(grad_half, key_head, preferred_element_type=jnp.float32) * scaling).astype(jnp.bfloat16)
        head_key_grad = jnp.dot(grad_half.T, query_head, preferred_element_type=jnp.float32) * scaling
        head_value_grad = jnp.dot(probs_half.T, cotangent_head, preferred_element_type=jnp.float32)
        head_logit_sum = lax.optimization_barrier(jnp.sum(jnp.where(delayed, score_grad, 0.0), axis=0))
        return (head_query_grad, head_key_grad, head_value_grad, head_logit_sum)
    query_grad, key_heads, value_heads, logit_heads = lax.map(per_head, jnp.arange(QH, dtype=jnp.int32))
    key_grad = lax.optimization_barrier(jnp.sum(key_heads.reshape(KVH, GROUP, TOKENS, HD), axis=1))
    value_grad = lax.optimization_barrier(jnp.sum(value_heads.reshape(KVH, GROUP, TOKENS, HD), axis=1))
    logit_grad = -jax.nn.sigmoid(evict_logits) * lax.optimization_barrier(jnp.sum(logit_heads.reshape(KVH, GROUP, TOKENS), axis=1))
    return (query_grad, key_grad, value_grad, logit_grad)
```

```python
import functools
import math

import jax
import jax.numpy as jnp
from jax import lax
from jax.experimental import pallas as pl
from jax.experimental.pallas import tpu as pltpu
from jax.sharding import Mesh, PartitionSpec as P

WINDOW = 256
HD = 128
HALF = 64
SHARD = 128
HEADS = 8
ROWS = HEADS * HALF
BLOCKS = 128
LOWEST = -1e30
SCALE = 1.0 / math.sqrt(HD)

NA = 4
NZ = 8
SLOTS = 2 * NZ
QB = 2 * NA
KV_ROWS = 2 * SHARD + 16

STEP = 4
CK = STEP * HALF
PER_BLOCK = SLOTS // STEP
TILES = [slice(j * SHARD, (j + 1) * SHARD) for j in range(ROWS // SHARD)]
WIDE = 256
WIDE_TILES = [slice(j * WIDE, (j + 1) * WIDE) for j in range(ROWS // WIDE)]
SKIP = 64
HIDDEN = 1000

QBLOCK_AT, SEEN_AT, SLOT_AT, POS_AT = 0, 1, 3, 5

NT = (((1,), (1,)), ((), ()))
NN = (((1,), (0,)), ((), ()))
f32, bf16, i32 = jnp.float32, jnp.bfloat16, jnp.int32


def dot(a, b, dims):
    return lax.dot_general(a, b, dims, preferred_element_type=f32)


def plan_of(blocks, y, z, xl):
    shape = (8, NA * NZ * 2)
    sub = lax.broadcasted_iota(i32, shape, 0)
    lane = lax.broadcasted_iota(i32, shape, 1)
    low = jnp.broadcast_to(blocks[0:1, :].astype(f32), shape)
    high = BLOCKS - 1.0 - low

    def picked(mask, value, axis=1):
        return jnp.sum(jnp.where(mask, value, 0.0), axis=axis, keepdims=True)

    q_low = picked(lane == ((y + (sub >> 1)) & (NA - 1)) * (2 * NZ) + z * 2 + xl, low)
    q_block = jnp.where((sub[:, :1] & 1) == 1, BLOCKS - 1.0 - q_low, q_low)
    columns = {QBLOCK_AT: q_block}
    for col in range(2):
        x = xl if col == 0 else 1 - xl
        here = ((lane >> 4) == y) & ((lane & 1) == x)
        columns[SEEN_AT + col] = picked(here & (low <= q_block), 1.0) + picked(here & (high <= q_block), 1.0)
        k_low = picked(here & (((lane >> 1) & (NZ - 1)) == sub), low)
        columns[SLOT_AT + col] = picked(here & (low < k_low), 1.0)
        rank = picked(k_low < low, 1.0, axis=0)
        columns[POS_AT + col] = picked(here & (rank == sub.astype(f32)), low)
    at = lax.broadcasted_iota(i32, (8, SHARD), 1)
    return sum(jnp.where(at == n, value, 0.0) for n, value in columns.items()).astype(i32)


def pack_kernel(where, k_ref, v_ref, logit_ref, blocks_ref, out_ref, plan_ref):
    plan_ref[...] = plan_of(blocks_ref[...], *where())
    logit = logit_ref[...]
    penalty = jnp.maximum(logit, 0.0) + jnp.log(1.0 + jnp.exp(-jnp.abs(logit)))
    upper = penalty.astype(bf16).astype(f32)
    tail = jnp.concatenate([upper, penalty - upper, jnp.zeros((14, SHARD), f32)], axis=0).astype(bf16)
    for j in range(NZ):
        out_ref[j, 0:SHARD, :] = k_ref[0]
        out_ref[j, SHARD : 2 * SHARD, :] = v_ref[0]
        out_ref[j, 2 * SHARD :, :] = tail


def cotangent_kernel(where, g0, g1, g2, g3, w_ref, out_ref, rows):
    @pl.when(pl.program_id(0) == 0)
    def _():
        xh, core = where()
        pieces = ((xh, core, g0), (1 - xh, core, g1), (xh, 1 - core, g2), (1 - xh, 1 - core, g3))
        for a, b, ref in pieces:
            rows[pl.ds(pl.multiple_of((a * 2 + b) * 32, 32), 32), :] = ref[...]

    cot = dot(rows[...], w_ref[...], NT).astype(bf16)
    for i in range(2):
        out_ref[i] = cot[:, i * HD : (i + 1) * HD]


def sort_keys(plan_ref, col, kv_ref, ks, vs, pen=None):
    for j in range(NZ):
        low = plan_ref[j, SLOT_AT + col]
        if pen is not None:
            rows = kv_ref[j, 2 * SHARD : 2 * SHARD + 16, :].astype(f32)
            penalty = jnp.broadcast_to(rows[0:1] + rows[1:2], (SHARD, SHARD)).T
        for half, slot in ((0, low), (1, SLOTS - 1 - low)):
            at = pl.ds(pl.multiple_of(slot * HALF, HALF), HALF)
            here = slice(half * HALF, (half + 1) * HALF)
            ks[at, :] = kv_ref[j, here, :]
            vs[at, :] = kv_ref[j, SHARD + half * HALF : SHARD + (half + 1) * HALF, :]
            if pen is not None:
                pen[at, :] = penalty[here, :]


def turn(src, dest):
    for i in range(SLOTS * HALF // SHARD):
        dest[i] = src[i * SHARD : (i + 1) * SHARD, :].astype(f32).T.astype(bf16)


def list_steps(plan_ref, col, pos, steps):
    for n in range(NZ):
        low = plan_ref[n, POS_AT + col]
        pos[n] = low
        pos[SLOTS - 1 - n] = BLOCKS - 1 - low
    count = jnp.int32(0)
    for rh in range(QB):
        groups = (plan_ref[rh, SEEN_AT + col] + STEP - 1) // STEP
        for c in range(PER_BLOCK):
            steps[count] = rh * PER_BLOCK + c
            count = count + (c < groups).astype(i32)
    last = steps[count - 1]
    for i in range(3):
        steps[count + i] = last + SKIP
    return count


def step_of(steps, t):
    v = steps[t]
    rh = (v // PER_BLOCK) % QB
    c = v % PER_BLOCK
    return v, rh, c, pl.ds(pl.multiple_of(c * CK, CK), CK)


def thresholds(plan_ref, pos, v, rh, c):
    q_block = plan_ref[rh, QBLOCK_AT]
    ahead = [(q_block - pos[c * STEP + i]) * HALF for i in range(STEP)]
    return [(jnp.where(v >= SKIP, HIDDEN, -d), WINDOW - d) for d in ahead]


def offsets():
    shape = (HALF, SHARD)
    return lax.broadcasted_iota(i32, shape, 1) % HALF - lax.broadcasted_iota(i32, shape, 0)


def block_rows(c, i):
    return pl.ds(pl.multiple_of(c * CK + i * HALF, HALF), HALF)


def turned_piece(ref, c):
    n = CK // SHARD
    return jnp.concatenate([ref[c * n + i] for i in range(n)], axis=1)


def load_rows(refs, dest):
    for r, ref in enumerate(refs):
        for half in range(2):
            dest[2 * r + half] = ref[:, half * HALF : (half + 1) * HALF, :].reshape(ROWS, HD)


def forward_kernel(col, plan_ref, *refs):
    if col == 0:
        rows_in, (kv_ref, o_ref, st_ref, peaks, exps, qs, qt), refs = refs[:4], refs[4:11], refs[11:]
    else:
        (qt, kv_ref, o_ref, st_ref, peaks, exps), refs = refs[:6], refs[6:]
    ks, vs, vt, pen, s_a, s_b, f_a, f_b, pos, steps = refs
    count = list_steps(plan_ref, col, pos, steps)
    if col == 0:
        load_rows(rows_in, qs)
        for rh in range(QB):
            qt[rh] = qs[rh].astype(f32).T.astype(bf16)
    sort_keys(plan_ref, col, kv_ref, ks, vs, pen)
    turn(vs, vt)
    o_ref[...] = jnp.zeros_like(o_ref)
    for rh in range(QB):
        st_ref[rh, 0:1, :] = jnp.full((1, ROWS), LOWEST, f32)
        st_ref[rh, 1:2, :] = jnp.zeros((1, ROWS), f32)
    exps[0] = jnp.zeros_like(exps[0])
    f_b[...] = jnp.ones_like(f_b)

    def score(t, s_ref):
        _, rh, _, at = step_of(steps, t)
        s_ref[...] = dot(ks[at, :], qt[rh], NN)

    def soften(t, s_ref, f_ref):
        v, rh, c, _ = step_of(steps, t)
        limits = thresholds(plan_ref, pos, v, rh, c)
        offset = offsets()
        for lanes in TILES:
            parts = []
            for i, (seen, late) in enumerate(limits):
                s = s_ref[i * HALF : (i + 1) * HALF, lanes] * SCALE
                s = s - jnp.where(offset >= late, pen[block_rows(c, i), :], 0.0)
                parts.append(jnp.where(offset >= seen, s, LOWEST))
            peak = st_ref[rh, 0:1, lanes]
            tops = functools.reduce(jnp.maximum, parts)
            new_peak = jnp.maximum(peak, jnp.max(tops, axis=0, keepdims=True))
            factor = jnp.exp(peak - new_peak)
            parts = [jnp.exp(s - new_peak) for s in parts]
            total = jnp.sum(sum(parts), axis=0, keepdims=True)
            for i, p in enumerate(parts):
                exps[t, i * HALF : (i + 1) * HALF, lanes] = p.astype(bf16)
            f_ref[0:1, lanes] = factor
            peaks[t, 0:1, lanes] = new_peak
            st_ref[rh, 0:1, lanes] = new_peak
            st_ref[rh, 1:2, lanes] = st_ref[rh, 1:2, lanes] * factor + total

    def attend(t, f_ref):
        _, rh, c, _ = step_of(steps, t)
        o_ref[rh] = o_ref[rh] * f_ref[0:1, :] + dot(turned_piece(vt, c), exps[t], NN)

    score(0, s_a)

    def pair(i, _):
        t = 2 * i
        attend(jnp.maximum(t - 1, 0), f_b)
        score(t + 1, s_b)
        soften(t, s_a, f_a)
        attend(t, f_a)
        score(t + 2, s_a)
        soften(t + 1, s_b, f_b)
        return 0

    pairs = (count + 1) // 2
    lax.fori_loop(0, pairs, pair, 0)
    attend(2 * pairs - 1, f_b)


def weigh_kernel(o0, st0, o1, st1, c0, c1, c2, c3, out_ref, cs, ct):
    for r, ref in enumerate((c0, c1, c2, c3)):
        for half in range(2):
            rh = 2 * r + half
            rows = ref[:, half * HALF : (half + 1) * HALF, :].reshape(ROWS, HD)
            cot = rows.astype(f32).T
            cs[rh] = rows
            ct[rh] = cot.astype(bf16)
            peak = jnp.maximum(st0[rh, 0:1, :], st1[rh, 0:1, :])
            f0, f1 = (jnp.exp(st[rh, 0:1, :] - peak) for st in (st0, st1))
            total = st0[rh, 1:2, :] * f0 + st1[rh, 1:2, :] * f1
            seen = total > 0.0
            weighted = jnp.sum(cot * (o0[rh] * f0 + o1[rh] * f1), axis=0, keepdims=True)
            safe = jnp.where(seen, total, 1.0)
            out_ref[rh : rh + 1, :] = jnp.where(seen, peak + jnp.log(safe), LOWEST)
            out_ref[QB + rh : QB + rh + 1, :] = weighted / safe


def merge_stats(pieces, stats):
    for r in range(NA):
        for half in range(2):
            rh = 2 * r + half
            parts = [(ref, 2 * ((r - t) % NA) + half) for t, ref in enumerate(pieces)]
            norms = [ref[n : n + 1, :] for ref, n in parts]
            means = [ref[QB + n : QB + n + 1, :] for ref, n in parts]
            peak = functools.reduce(jnp.maximum, norms)
            shares = [jnp.exp(norm - peak) for norm in norms]
            total = sum(shares)
            stats[rh, 0:1, :] = peak + jnp.log(total)
            stats[rh, 1:2, :] = sum(share * mean for share, mean in zip(shares, means)) / total


def backward_kernel(col, plan_ref, *refs):
    (qs, cs, ct, kv_ref, peaks, exps), pieces, refs = refs[:6], refs[6:10], refs[10:]
    if col == 1:
        (dq, dkv_ref), refs = refs[:2], refs[2:]
    else:
        (dq_before,), dq_out, (dkv_ref,), refs = refs[:1], refs[1:5], refs[5:6], refs[6:]
        (dq, turned, sems), refs = refs[:3], refs[3:]
    ks, vs, kt, dk, dv, dl, stats, p_a, p_b, d_a, d_b, pos, steps = refs
    count = list_steps(plan_ref, col, pos, steps)
    sort_keys(plan_ref, col, kv_ref, ks, vs)
    turn(ks, kt)
    for ref in (dk, dv, dl, p_b, d_b):
        ref[...] = jnp.zeros_like(ref)
    dq[...] = jnp.zeros_like(dq) if col == 1 else dq_before[...]
    merge_stats(pieces, stats)

    def differ(t, p_ref, d_ref):
        v, rh, c, _ = step_of(steps, t)
        offset = offsets()
        shares = [jnp.exp(peaks[t, 0:1, lanes] - stats[rh, 0:1, lanes]) for lanes in TILES]
        for i, (_, late) in enumerate(thresholds(plan_ref, pos, v, rh, c)):
            at = block_rows(c, i)
            rows = slice(i * HALF, (i + 1) * HALF)
            delayed = offset >= late
            late_sum = dl[at, :]
            for wide in WIDE_TILES:
                grad = dot(vs[at, :], ct[rh, :, wide], NN)
                for j in range(WIDE // SHARD):
                    here = slice(j * SHARD, (j + 1) * SHARD)
                    lanes = slice(wide.start + here.start, wide.start + here.stop)
                    p = exps[t, rows, lanes].astype(f32) * shares[lanes.start // SHARD]
                    d = p * (grad[:, here] - stats[rh, 1:2, lanes])
                    late_sum = late_sum + jnp.where(delayed, d, 0.0)
                    p_ref[rows, lanes] = p.astype(bf16)
                    d_ref[rows, lanes] = d.astype(bf16)
            dl[at, :] = late_sum

    def gather(t, p_ref, d_ref):
        _, rh, c, at = step_of(steps, t)
        dk[at, :] += dot(d_ref[...], qs[rh], NN)
        dv[at, :] += dot(p_ref[...], cs[rh], NN)
        dq[rh] += dot(turned_piece(kt, c), d_ref[...], NN)

    def pair(i, _):
        t = 2 * i
        gather(jnp.maximum(t - 1, 0), p_b, d_b)
        differ(t, p_a, d_a)
        gather(t, p_a, d_a)
        differ(t + 1, p_b, d_b)
        return 0

    pairs = (count + 1) // 2
    lax.fori_loop(0, pairs, pair, 0)
    gather(2 * pairs - 1, p_b, d_b)
    copies = []
    if col == 0:
        for r, ref in enumerate(dq_out):
            for half in range(2):
                rows = (dq[2 * r + half].T * SCALE).astype(bf16)
                turned[r, :, half * HALF : (half + 1) * HALF, :] = rows.reshape(HEADS, HALF, HD)
            copies.append(pltpu.make_async_copy(turned.at[r], ref, sems.at[r]))
            copies[-1].start()
    for j in range(NZ):
        low = plan_ref[j, SLOT_AT + col]
        spots = [pl.ds(pl.multiple_of(slot * HALF, HALF), HALF) for slot in (low, SLOTS - 1 - low)]
        for half, at in enumerate(spots):
            dkv_ref[j, half * HALF : (half + 1) * HALF, :] = (dk[at, :] * SCALE).astype(dkv_ref.dtype)
            dkv_ref[j, SHARD + half * HALF : SHARD + (half + 1) * HALF, :] = dv[at, :].astype(dkv_ref.dtype)
        late = jnp.concatenate([dl[at, :] for at in spots], axis=0)
        total = jnp.sum(late.T, axis=0, keepdims=True)
        dkv_ref[j, 2 * SHARD : 2 * SHARD + 16, :] = jnp.concatenate(
            [total, jnp.zeros((15, SHARD), f32)], axis=0
        ).astype(dkv_ref.dtype)
    for copy in copies:
        copy.wait()


VMEM = pl.BlockSpec(memory_space=pltpu.VMEM)
SMEM = pl.BlockSpec(memory_space=pltpu.SMEM)
HBM = pl.BlockSpec(memory_space=pltpu.HBM)


def grant(mib):
    return pltpu.CompilerParams(vmem_limit_bytes=mib * 1024 * 1024)


MOST = 5 * NA
ROOMY = grant(54)
KEYS = SLOTS * HALF
shaped = jax.ShapeDtypeStruct


def cost(us):
    return pl.CostEstimate(flops=int(us * 1e9), bytes_accessed=2**20, transcendentals=0)


def run_pack(where, keys, values, logits, block_order):
    return pl.pallas_call(
        functools.partial(pack_kernel, where),
        out_shape=(shaped((NZ, KV_ROWS, HD), bf16), shaped((8, SHARD), i32)),
        in_specs=[VMEM] * 4,
        out_specs=(VMEM, VMEM),
        name="pack",
    )(keys, values, logits, block_order.T)


def run_cotangent(where, pieces, w_out):
    rows, width = w_out.shape
    return pl.pallas_call(
        functools.partial(cotangent_kernel, where),
        out_shape=shaped((HEADS, SHARD, HD), bf16),
        grid=(HEADS // 2,),
        in_specs=[pl.BlockSpec((32, width), lambda i: (0, 0))] * 4
        + [pl.BlockSpec((2 * HD, width), lambda i: (i, 0))],
        out_specs=pl.BlockSpec((2, SHARD, HD), lambda i: (i, 0, 0)),
        scratch_shapes=[pltpu.VMEM((SHARD, width), bf16)],
        compiler_params=ROOMY,
        cost_estimate=cost(5),
        name="cotangent",
    )(*pieces, w_out)


def run_forward(col, plan, q, kv):
    out_shape = (
        shaped((QB, HD, ROWS), f32),
        shaped((QB, 2, ROWS), f32),
        shaped((MOST, 1, ROWS), f32),
        shaped((MOST, CK, ROWS), bf16),
    )
    if col == 0:
        out_shape += (shaped((QB, ROWS, HD), bf16), shaped((QB, HD, ROWS), bf16))
    o, st, peaks, exps, *turned = pl.pallas_call(
        functools.partial(forward_kernel, col),
        out_shape=out_shape,
        in_specs=[SMEM] + [VMEM] * (len(q) + 1),
        out_specs=(VMEM,) * len(out_shape),
        scratch_shapes=[
            pltpu.VMEM((KEYS, HD), bf16),
            pltpu.VMEM((KEYS, HD), bf16),
            pltpu.VMEM((KEYS // SHARD, HD, SHARD), bf16),
            pltpu.VMEM((KEYS, SHARD), f32),
            pltpu.VMEM((CK, ROWS), f32),
            pltpu.VMEM((CK, ROWS), f32),
            pltpu.VMEM((8, ROWS), f32),
            pltpu.VMEM((8, ROWS), f32),
            pltpu.SMEM((SLOTS,), i32),
            pltpu.SMEM((QB * PER_BLOCK + 3,), i32),
        ],
        compiler_params=grant(14),
        cost_estimate=cost(10),
        name=f"forward{col}",
    )(plan, *q, kv)
    return (o, st), (peaks, exps), turned


def run_weigh(sums, cot):
    return pl.pallas_call(
        weigh_kernel,
        out_shape=(
            shaped((2 * QB, ROWS), f32),
            shaped((QB, ROWS, HD), bf16),
            shaped((QB, HD, ROWS), bf16),
        ),
        in_specs=[VMEM] * 8,
        out_specs=(VMEM,) * 3,
        compiler_params=grant(8),
        name="weigh",
    )(*sums, *cot)


def run_backward(col, plan, rows, kv, exps, stats, dq_sum=None):
    if col == 1:
        more, scratch = (), []
        out_shape = (shaped((QB, HD, ROWS), f32), shaped((NZ, KV_ROWS, HD), bf16))
        out_specs = (VMEM, VMEM)
    else:
        more = (dq_sum,)
        scratch = [
            pltpu.VMEM((QB, HD, ROWS), f32),
            pltpu.VMEM((NA, HEADS, SHARD, HD), bf16),
            pltpu.SemaphoreType.DMA((NA,)),
        ]
        out_shape = (shaped((HEADS, SHARD, HD), bf16),) * NA + (shaped((NZ, KV_ROWS, HD), f32),)
        out_specs = (HBM,) * NA + (VMEM,)
    return pl.pallas_call(
        functools.partial(backward_kernel, col),
        out_shape=out_shape,
        in_specs=[SMEM] + [VMEM] * (10 + len(more)),
        out_specs=out_specs,
        scratch_shapes=scratch
        + [
            pltpu.VMEM((KEYS, HD), bf16),
            pltpu.VMEM((KEYS, HD), bf16),
            pltpu.VMEM((KEYS // SHARD, HD, SHARD), bf16),
            pltpu.VMEM((KEYS, HD), f32),
            pltpu.VMEM((KEYS, HD), f32),
            pltpu.VMEM((KEYS, SHARD), f32),
            pltpu.VMEM((QB, 2, ROWS), f32),
        ]
        + [pltpu.VMEM((CK, ROWS), bf16)] * 4
        + [pltpu.SMEM((SLOTS,), i32), pltpu.SMEM((QB * PER_BLOCK + 3,), i32)],
        compiler_params=grant(18),
        cost_estimate=cost(15),
        name=f"backward{col}",
    )(plan, *rows, kv, *exps, *stats, *more)


def from_y(x, r):
    return lax.ppermute(x, "y", [((i + r) % NA, i) for i in range(NA)])


def gather_y(x):
    return [x] + [from_y(x, r) for r in range(1, NA)]


def swap(x, axis):
    return lax.ppermute(x, axis, [(0, 1), (1, 0)])


def place():
    return lax.axis_index("y"), lax.axis_index("z"), lax.axis_index("xl")


def head_place():
    return lax.axis_index("xh"), lax.axis_index("core")


def per_device(queries, keys, values, evict_logits, block_order, grad_y, w_out):
    packed, plan = run_pack(place, keys, values, evict_logits, block_order)
    kv = lax.all_to_all(packed, "z", 0, 0, tiled=True)
    over = swap(grad_y, "xh")
    pieces = (grad_y, over, swap(grad_y, "core"), swap(over, "core"))
    q_all = gather_y(queries)
    cot = run_cotangent(head_place, pieces, w_out)
    kv_other = swap(kv, "xl")
    cot_all = gather_y(cot)
    sums0, exps0, (qs, qt) = run_forward(0, plan, q_all, kv)
    sums1, exps1, _ = run_forward(1, plan, (qt,), kv_other)
    stats, cs, ct = run_weigh((*sums0, *sums1), cot_all)
    rows = (qs, cs, ct)
    stats = gather_y(stats)
    dq_sum, dkv_other = run_backward(1, plan, rows, kv_other, exps1, stats)
    dkv_here = swap(dkv_other, "xl")
    *dq, dkv = run_backward(0, plan, rows, kv, exps0, stats, dq_sum)
    dkv = (dkv + dkv_here.astype(f32)).astype(bf16)
    dkv = jnp.sum(lax.all_to_all(dkv, "z", 0, 0, tiled=True).astype(f32), axis=0)
    query_grad = dq[0].astype(f32)
    for r in range(1, NA):
        query_grad = query_grad + from_y(dq[r], NA - r).astype(f32)
    logit_grad = -jax.nn.sigmoid(evict_logits[0]) * dkv[2 * SHARD]
    return (
        query_grad.astype(bf16),
        dkv[None, :SHARD],
        dkv[None, SHARD : 2 * SHARD],
        logit_grad[None],
    )


def solution(mesh):
    split = Mesh(mesh.devices.reshape(4, 8, 2, 2, 2), ("y", "z", "xl", "xh", "core"))
    ctx, head = ("y", "z", "xl"), ("xh", "core")
    return jax.shard_map(
        per_device,
        mesh=split,
        in_specs=(
            P(head, ctx, None),
            P(head, ctx, None),
            P(head, ctx, None),
            P(head, ctx),
            P(),
            P(ctx + head, None),
            P(head, None),
        ),
        out_specs=(
            P(head, ctx, None),
            P(head, ctx, None),
            P(head, ctx, None),
            P(head, ctx),
        ),
        check_vma=False,
    )
```

```python
import functools
import math

import jax
import jax.numpy as jnp
from jax import lax
from jax.experimental import pallas as pl
from jax.experimental.pallas import tpu as pltpu
from jax.sharding import Mesh, PartitionSpec as P

WINDOW = 256
HD = 128
HALF = 64
SHARD = 128
HEADS = 8
ROWS = HEADS * HALF
BLOCKS = 128
LOWEST = -1e30
SCALE = 1.0 / math.sqrt(HD)

NA = 4
NZ = 8
SLOTS = 2 * NZ
QB = 2 * NA
KV_ROWS = 2 * SHARD + 16

STEP = 4
CK = STEP * HALF
PER_BLOCK = SLOTS // STEP
TILES = [slice(j * SHARD, (j + 1) * SHARD) for j in range(ROWS // SHARD)]
WIDE = 256
WIDE_TILES = [slice(j * WIDE, (j + 1) * WIDE) for j in range(ROWS // WIDE)]
SKIP = 64
HIDDEN = 1000

QBLOCK_AT, SEEN_AT, SLOT_AT, POS_AT, FAR_AT = 0, 1, 3, 5, 7
FAR = (WINDOW + 2 * HALF - 2) // HALF

NT = (((1,), (1,)), ((), ()))
NN = (((1,), (0,)), ((), ()))
f32, bf16, i32 = jnp.float32, jnp.bfloat16, jnp.int32


def dot(a, b, dims):
    return lax.dot_general(a, b, dims, preferred_element_type=f32)


def plan_of(blocks, y, z, xl):
    shape = (8, NA * NZ * 2)
    sub = lax.broadcasted_iota(i32, shape, 0)
    lane = lax.broadcasted_iota(i32, shape, 1)
    low = jnp.broadcast_to(blocks[0:1, :].astype(f32), shape)
    high = BLOCKS - 1.0 - low

    def picked(mask, value, axis=1):
        return jnp.sum(jnp.where(mask, value, 0.0), axis=axis, keepdims=True)

    q_low = picked(lane == ((y + (sub >> 1)) & (NA - 1)) * (2 * NZ) + z * 2 + xl, low)
    q_block = jnp.where((sub[:, :1] & 1) == 1, BLOCKS - 1.0 - q_low, q_low)
    columns = {QBLOCK_AT: q_block}
    for col in range(2):
        x = xl if col == 0 else 1 - xl
        here = ((lane >> 4) == y) & ((lane & 1) == x)
        columns[SEEN_AT + col] = picked(here & (low <= q_block), 1.0) + picked(here & (high <= q_block), 1.0)
        far = q_block - FAR
        columns[FAR_AT + col] = picked(here & (low <= far), 1.0) + picked(here & (high <= far), 1.0)
        k_low = picked(here & (((lane >> 1) & (NZ - 1)) == sub), low)
        columns[SLOT_AT + col] = picked(here & (low < k_low), 1.0)
        rank = picked(k_low < low, 1.0, axis=0)
        columns[POS_AT + col] = picked(here & (rank == sub.astype(f32)), low)
    at = lax.broadcasted_iota(i32, (8, SHARD), 1)
    return sum(jnp.where(at == n, value, 0.0) for n, value in columns.items()).astype(i32)


def plan_kernel(where, blocks_ref, plan_ref):
    plan_ref[...] = plan_of(blocks_ref[...], *where())


def pack_kernel(k_ref, v_ref, logit_ref, out_ref):
    logit = logit_ref[...]
    penalty = jnp.maximum(logit, 0.0) + jnp.log(1.0 + jnp.exp(-jnp.abs(logit)))
    upper = penalty.astype(bf16).astype(f32)
    tail = jnp.concatenate([upper, penalty - upper, jnp.zeros((14, SHARD), f32)], axis=0).astype(bf16)
    for j in range(NZ):
        out_ref[j, 0:SHARD, :] = k_ref[0]
        out_ref[j, SHARD : 2 * SHARD, :] = v_ref[0]
        out_ref[j, 2 * SHARD :, :] = tail


def cotangent_kernel(where, g0, g1, g2, g3, w_ref, out_ref, rows):
    xh, core = where()
    pieces = ((xh, core, g0), (1 - xh, core, g1), (xh, 1 - core, g2), (1 - xh, 1 - core, g3))
    for a, b, ref in pieces:
        rows[pl.ds(pl.multiple_of((a * 2 + b) * 32, 32), 32), :] = ref[...]
    for i in range(0, HEADS, 2):
        cot = dot(rows[...], w_ref[i * HD : (i + 2) * HD, :], NT).astype(bf16)
        out_ref[i] = cot[:, :HD]
        out_ref[i + 1] = cot[:, HD:]


def sort_keys(plan_ref, col, kv_ref, ks, vs, pen=None):
    for j in range(NZ):
        low = plan_ref[j, SLOT_AT + col]
        if pen is not None:
            rows = kv_ref[j, 2 * SHARD : 2 * SHARD + 16, :].astype(f32)
            penalty = jnp.broadcast_to(rows[0:1] + rows[1:2], (SHARD, SHARD)).T
        for half, slot in ((0, low), (1, SLOTS - 1 - low)):
            at = pl.ds(pl.multiple_of(slot * HALF, HALF), HALF)
            here = slice(half * HALF, (half + 1) * HALF)
            ks[at, :] = kv_ref[j, here, :]
            vs[at, :] = kv_ref[j, SHARD + half * HALF : SHARD + (half + 1) * HALF, :]
            if pen is not None:
                pen[at, :] = penalty[here, :]


def turn(src, dest):
    for i in range(SLOTS * HALF // SHARD):
        dest[i] = src[i * SHARD : (i + 1) * SHARD, :].astype(f32).T.astype(bf16)


def list_steps(plan_ref, col, pos, steps):
    for n in range(NZ):
        low = plan_ref[n, POS_AT + col]
        pos[n] = low
        pos[SLOTS - 1 - n] = BLOCKS - 1 - low
    count = jnp.int32(0)
    far = [plan_ref[rh, FAR_AT + col] // STEP for rh in range(QB)]
    for rh in range(QB):
        for c in range(PER_BLOCK):
            steps[count] = rh * PER_BLOCK + c
            count = count + (c < far[rh]).astype(i32)
    plain = count
    for rh in range(QB):
        groups = (plan_ref[rh, SEEN_AT + col] + STEP - 1) // STEP
        for c in range(PER_BLOCK):
            steps[count] = rh * PER_BLOCK + c
            count = count + ((c >= far[rh]) & (c < groups)).astype(i32)
    last = steps[count - 1]
    for i in range(3):
        steps[count + i] = last + SKIP
    return plain, count


def step_of(steps, t):
    v = steps[t]
    rh = (v // PER_BLOCK) % QB
    c = v % PER_BLOCK
    return v, rh, c, pl.ds(pl.multiple_of(c * CK, CK), CK)


def thresholds(plan_ref, pos, v, rh, c):
    q_block = plan_ref[rh, QBLOCK_AT]
    ahead = [(q_block - pos[c * STEP + i]) * HALF for i in range(STEP)]
    return [(jnp.where(v >= SKIP, HIDDEN, -d), WINDOW - d) for d in ahead]


def offsets():
    shape = (HALF, SHARD)
    return lax.broadcasted_iota(i32, shape, 1) % HALF - lax.broadcasted_iota(i32, shape, 0)


def block_rows(c, i):
    return pl.ds(pl.multiple_of(c * CK + i * HALF, HALF), HALF)


def turned_piece(ref, c):
    n = CK // SHARD
    return jnp.concatenate([ref[c * n + i] for i in range(n)], axis=1)


def load_rows(refs, dest):
    for r, ref in enumerate(refs):
        for half in range(2):
            dest[2 * r + half] = ref[:, half * HALF : (half + 1) * HALF, :].reshape(ROWS, HD)


def forward_kernel(col, plan_ref, *refs):
    if col == 0:
        rows_in, (kv_ref, o_ref, st_ref, peaks, exps, qs, qt), refs = refs[:4], refs[4:11], refs[11:]
    else:
        (qt, kv_ref, o_ref, st_ref, peaks, exps), refs = refs[:6], refs[6:]
    ks, vs, vt, pen, s_a, s_b, f_a, f_b, pos, steps = refs
    plain, count = list_steps(plan_ref, col, pos, steps)
    if col == 0:
        load_rows(rows_in, qs)
        for rh in range(QB):
            qt[rh] = qs[rh].astype(f32).T.astype(bf16)
    sort_keys(plan_ref, col, kv_ref, ks, vs, pen)
    turn(vs, vt)
    o_ref[...] = jnp.zeros_like(o_ref)
    for rh in range(QB):
        st_ref[rh, 0:1, :] = jnp.full((1, ROWS), LOWEST, f32)
        st_ref[rh, 1:2, :] = jnp.zeros((1, ROWS), f32)
    exps[0] = jnp.zeros_like(exps[0])
    f_b[...] = jnp.ones_like(f_b)

    def score(t, s_ref):
        _, rh, _, at = step_of(steps, t)
        s_ref[...] = dot(ks[at, :], qt[rh], NN)

    def soften(t, s_ref, f_ref, masked):
        v, rh, c, _ = step_of(steps, t)
        limits = thresholds(plan_ref, pos, v, rh, c)
        offset = offsets()
        for lanes in TILES:
            parts = []
            for i, (seen, late) in enumerate(limits):
                s = s_ref[i * HALF : (i + 1) * HALF, lanes] * SCALE
                penalty = pen[block_rows(c, i), :]
                if masked:
                    s = s - jnp.where(offset >= late, penalty, 0.0)
                    parts.append(jnp.where(offset >= seen, s, LOWEST))
                else:
                    parts.append(s - penalty)
            peak = st_ref[rh, 0:1, lanes]
            tops = functools.reduce(jnp.maximum, parts)
            new_peak = jnp.maximum(peak, jnp.max(tops, axis=0, keepdims=True))
            factor = jnp.exp(peak - new_peak)
            parts = [jnp.exp(s - new_peak) for s in parts]
            total = jnp.sum(sum(parts), axis=0, keepdims=True)
            for i, p in enumerate(parts):
                exps[t, i * HALF : (i + 1) * HALF, lanes] = p.astype(bf16)
            f_ref[0:1, lanes] = factor
            peaks[t, 0:1, lanes] = new_peak
            st_ref[rh, 0:1, lanes] = new_peak
            st_ref[rh, 1:2, lanes] = st_ref[rh, 1:2, lanes] * factor + total

    def attend(t, f_ref):
        _, rh, c, _ = step_of(steps, t)
        o_ref[rh] = o_ref[rh] * f_ref[0:1, :] + dot(turned_piece(vt, c), exps[t], NN)

    score(0, s_a)

    def pair(masked, i, _):
        t = 2 * i
        attend(jnp.maximum(t - 1, 0), f_b)
        score(t + 1, s_b)
        soften(t, s_a, f_a, masked)
        attend(t, f_a)
        score(t + 2, s_a)
        soften(t + 1, s_b, f_b, masked)
        return 0

    pairs = (count + 1) // 2
    lax.fori_loop(0, plain // 2, functools.partial(pair, False), 0)
    lax.fori_loop(plain // 2, pairs, functools.partial(pair, True), 0)
    attend(2 * pairs - 1, f_b)


def weigh_kernel(o0, st0, o1, st1, c0, c1, c2, c3, out_ref, cs, ct):
    for r, ref in enumerate((c0, c1, c2, c3)):
        for half in range(2):
            rh = 2 * r + half
            rows = ref[:, half * HALF : (half + 1) * HALF, :].reshape(ROWS, HD)
            cot = rows.astype(f32).T
            cs[rh] = rows
            ct[rh] = cot.astype(bf16)
            peak = jnp.maximum(st0[rh, 0:1, :], st1[rh, 0:1, :])
            f0, f1 = (jnp.exp(st[rh, 0:1, :] - peak) for st in (st0, st1))
            total = st0[rh, 1:2, :] * f0 + st1[rh, 1:2, :] * f1
            seen = total > 0.0
            weighted = jnp.sum(cot * (o0[rh] * f0 + o1[rh] * f1), axis=0, keepdims=True)
            safe = jnp.where(seen, total, 1.0)
            out_ref[rh : rh + 1, :] = jnp.where(seen, peak + jnp.log(safe), LOWEST)
            out_ref[QB + rh : QB + rh + 1, :] = weighted / safe


def merge_stats(pieces, stats):
    for r in range(NA):
        for half in range(2):
            rh = 2 * r + half
            parts = [(ref, 2 * ((r - t) % NA) + half) for t, ref in enumerate(pieces)]
            norms = [ref[n : n + 1, :] for ref, n in parts]
            means = [ref[QB + n : QB + n + 1, :] for ref, n in parts]
            peak = functools.reduce(jnp.maximum, norms)
            shares = [jnp.exp(norm - peak) for norm in norms]
            total = sum(shares)
            stats[rh, 0:1, :] = peak + jnp.log(total)
            stats[rh, 1:2, :] = sum(share * mean for share, mean in zip(shares, means)) / total


def backward_kernel(col, plan_ref, *refs):
    (qs, cs, ct, kv_ref, peaks, exps), pieces, refs = refs[:6], refs[6:10], refs[10:]
    if col == 1:
        (dq, dkv_ref), refs = refs[:2], refs[2:]
    else:
        (dq_before,), dq_out, (dkv_ref,), refs = refs[:1], refs[1:5], refs[5:6], refs[6:]
        (dq, turned, sems), refs = refs[:3], refs[3:]
    ks, vs, kt, dk, dv, dl, stats, p_a, p_b, d_a, d_b, pos, steps = refs
    plain, count = list_steps(plan_ref, col, pos, steps)
    sort_keys(plan_ref, col, kv_ref, ks, vs)
    turn(ks, kt)
    for ref in (dk, dv, dl, p_b, d_b):
        ref[...] = jnp.zeros_like(ref)
    dq[...] = jnp.zeros_like(dq) if col == 1 else dq_before[...]
    merge_stats(pieces, stats)

    def differ(t, p_ref, d_ref, masked):
        v, rh, c, _ = step_of(steps, t)
        offset = offsets()
        limits = thresholds(plan_ref, pos, v, rh, c)
        shares = [jnp.exp(peaks[t, 0:1, lanes] - stats[rh, 0:1, lanes]) for lanes in TILES]
        for first in range(0, STEP, 2):
            blocks = (first, first + 1)
            late_sums = [dl[block_rows(c, i), :] for i in blocks]
            at = pl.ds(pl.multiple_of(c * CK + first * HALF, SHARD), 2 * HALF)
            for wide in WIDE_TILES:
                grad = dot(vs[at, :], ct[rh, :, wide], NN)
                for n, i in enumerate(blocks):
                    rows = slice(i * HALF, (i + 1) * HALF)
                    for j in range(WIDE // SHARD):
                        here = slice(j * SHARD, (j + 1) * SHARD)
                        lanes = slice(wide.start + here.start, wide.start + here.stop)
                        p = exps[t, rows, lanes].astype(f32) * shares[lanes.start // SHARD]
                        d = p * (grad[n * HALF : (n + 1) * HALF, here] - stats[rh, 1:2, lanes])
                        late = jnp.where(offset >= limits[i][1], d, 0.0) if masked else d
                        late_sums[n] = late_sums[n] + late
                        p_ref[rows, lanes] = p.astype(bf16)
                        d_ref[rows, lanes] = d.astype(bf16)
            for n, i in enumerate(blocks):
                dl[block_rows(c, i), :] = late_sums[n]

    def gather(t, p_ref, d_ref):
        _, rh, c, at = step_of(steps, t)
        dk[at, :] += dot(d_ref[...], qs[rh], NN)
        dv[at, :] += dot(p_ref[...], cs[rh], NN)
        dq[rh] += dot(turned_piece(kt, c), d_ref[...], NN)

    def pair(masked, i, _):
        t = 2 * i
        gather(jnp.maximum(t - 1, 0), p_b, d_b)
        differ(t, p_a, d_a, masked)
        gather(t, p_a, d_a)
        differ(t + 1, p_b, d_b, masked)
        return 0

    pairs = (count + 1) // 2
    lax.fori_loop(0, plain // 2, functools.partial(pair, False), 0)
    lax.fori_loop(plain // 2, pairs, functools.partial(pair, True), 0)
    gather(2 * pairs - 1, p_b, d_b)
    copies = []
    if col == 0:
        for r, ref in enumerate(dq_out):
            for half in range(2):
                rows = (dq[2 * r + half].T * SCALE).astype(bf16)
                turned[r, :, half * HALF : (half + 1) * HALF, :] = rows.reshape(HEADS, HALF, HD)
            copies.append(pltpu.make_async_copy(turned.at[r], ref, sems.at[r]))
            copies[-1].start()
    for j in range(NZ):
        low = plan_ref[j, SLOT_AT + col]
        spots = [pl.ds(pl.multiple_of(slot * HALF, HALF), HALF) for slot in (low, SLOTS - 1 - low)]
        for half, at in enumerate(spots):
            dkv_ref[j, half * HALF : (half + 1) * HALF, :] = (dk[at, :] * SCALE).astype(dkv_ref.dtype)
            dkv_ref[j, SHARD + half * HALF : SHARD + (half + 1) * HALF, :] = dv[at, :].astype(dkv_ref.dtype)
        late = jnp.concatenate([dl[at, :] for at in spots], axis=0)
        total = jnp.sum(late.T, axis=0, keepdims=True)
        dkv_ref[j, 2 * SHARD : 2 * SHARD + 16, :] = jnp.concatenate(
            [total, jnp.zeros((15, SHARD), f32)], axis=0
        ).astype(dkv_ref.dtype)
    for copy in copies:
        copy.wait()


def total_kernel(parts_ref, logit_ref, dk_ref, dv_ref, dl_ref):
    total = parts_ref[0].astype(f32)
    for n in range(1, NZ):
        total = total + parts_ref[n].astype(f32)
    dk_ref[0] = total[:SHARD]
    dv_ref[0] = total[SHARD : 2 * SHARD]
    dl_ref[...] = -jax.nn.sigmoid(logit_ref[...]) * total[2 * SHARD : 2 * SHARD + 1]


VMEM = pl.BlockSpec(memory_space=pltpu.VMEM)
SMEM = pl.BlockSpec(memory_space=pltpu.SMEM)
HBM = pl.BlockSpec(memory_space=pltpu.HBM)


def grant(mib):
    return pltpu.CompilerParams(vmem_limit_bytes=mib * 1024 * 1024)


MOST = 5 * NA
KEYS = SLOTS * HALF
shaped = jax.ShapeDtypeStruct


def cost(us):
    return pl.CostEstimate(flops=int(us * 1e9), bytes_accessed=2**20, transcendentals=0)


def run_plan(where, block_order):
    return pl.pallas_call(
        functools.partial(plan_kernel, where),
        out_shape=shaped((8, SHARD), i32),
        in_specs=[VMEM],
        out_specs=VMEM,
        compiler_params=grant(4),
        cost_estimate=cost(12),
        name="plan",
    )(block_order.T)


def run_pack(keys, values, logits):
    return pl.pallas_call(
        pack_kernel,
        out_shape=shaped((NZ, KV_ROWS, HD), bf16),
        in_specs=[VMEM] * 3,
        out_specs=VMEM,
        compiler_params=grant(4),
        name="pack",
    )(keys, values, logits)


def run_cotangent(where, pieces, w_out):
    return pl.pallas_call(
        functools.partial(cotangent_kernel, where),
        out_shape=shaped((HEADS, SHARD, HD), bf16),
        in_specs=[VMEM] * 5,
        out_specs=VMEM,
        scratch_shapes=[pltpu.VMEM((SHARD, w_out.shape[1]), bf16)],
        compiler_params=grant(8),
        cost_estimate=cost(5),
        name="cotangent",
    )(*pieces, w_out)


def run_forward(col, plan, q, kv):
    out_shape = (
        shaped((QB, HD, ROWS), f32),
        shaped((QB, 2, ROWS), f32),
        shaped((MOST, 1, ROWS), f32),
        shaped((MOST, CK, ROWS), bf16),
    )
    if col == 0:
        out_shape += (shaped((QB, ROWS, HD), bf16), shaped((QB, HD, ROWS), bf16))
    o, st, peaks, exps, *turned = pl.pallas_call(
        functools.partial(forward_kernel, col),
        out_shape=out_shape,
        in_specs=[SMEM] + [VMEM] * (len(q) + 1),
        out_specs=(VMEM,) * len(out_shape),
        scratch_shapes=[
            pltpu.VMEM((KEYS, HD), bf16),
            pltpu.VMEM((KEYS, HD), bf16),
            pltpu.VMEM((KEYS // SHARD, HD, SHARD), bf16),
            pltpu.VMEM((KEYS, SHARD), f32),
            pltpu.VMEM((CK, ROWS), f32),
            pltpu.VMEM((CK, ROWS), f32),
            pltpu.VMEM((8, ROWS), f32),
            pltpu.VMEM((8, ROWS), f32),
            pltpu.SMEM((SLOTS,), i32),
            pltpu.SMEM((QB * PER_BLOCK + 3,), i32),
        ],
        compiler_params=grant(14),
        cost_estimate=cost(10),
        name=f"forward{col}",
    )(plan, *q, kv)
    return (o, st), (peaks, exps), turned


def run_weigh(sums, cot):
    return pl.pallas_call(
        weigh_kernel,
        out_shape=(
            shaped((2 * QB, ROWS), f32),
            shaped((QB, ROWS, HD), bf16),
            shaped((QB, HD, ROWS), bf16),
        ),
        in_specs=[VMEM] * 8,
        out_specs=(VMEM,) * 3,
        compiler_params=grant(8),
        name="weigh",
    )(*sums, *cot)


def run_backward(col, plan, rows, kv, exps, stats, dq_sum=None):
    if col == 1:
        more, scratch = (), []
        out_shape = (shaped((QB, HD, ROWS), f32), shaped((NZ, KV_ROWS, HD), bf16))
        out_specs = (VMEM, VMEM)
    else:
        more = (dq_sum,)
        scratch = [
            pltpu.VMEM((QB, HD, ROWS), f32),
            pltpu.VMEM((NA, HEADS, SHARD, HD), bf16),
            pltpu.SemaphoreType.DMA((NA,)),
        ]
        out_shape = (shaped((HEADS, SHARD, HD), bf16),) * NA + (shaped((NZ, KV_ROWS, HD), f32),)
        out_specs = (HBM,) * NA + (VMEM,)
    return pl.pallas_call(
        functools.partial(backward_kernel, col),
        out_shape=out_shape,
        in_specs=[SMEM] + [VMEM] * (10 + len(more)),
        out_specs=out_specs,
        scratch_shapes=scratch
        + [
            pltpu.VMEM((KEYS, HD), bf16),
            pltpu.VMEM((KEYS, HD), bf16),
            pltpu.VMEM((KEYS // SHARD, HD, SHARD), bf16),
            pltpu.VMEM((KEYS, HD), f32),
            pltpu.VMEM((KEYS, HD), f32),
            pltpu.VMEM((KEYS, SHARD), f32),
            pltpu.VMEM((QB, 2, ROWS), f32),
        ]
        + [pltpu.VMEM((CK, ROWS), bf16)] * 4
        + [pltpu.SMEM((SLOTS,), i32), pltpu.SMEM((QB * PER_BLOCK + 3,), i32)],
        compiler_params=grant(18),
        cost_estimate=cost(15),
        name=f"backward{col}",
    )(plan, *rows, kv, *exps, *stats, *more)


def run_total(parts, logits):
    return pl.pallas_call(
        total_kernel,
        out_shape=(shaped((1, SHARD, HD), f32), shaped((1, SHARD, HD), f32), shaped((1, SHARD), f32)),
        in_specs=[VMEM] * 2,
        out_specs=(VMEM,) * 3,
        compiler_params=grant(4),
        name="total",
    )(parts, logits)


def from_y(x, r):
    return lax.ppermute(x, "y", [((i + r) % NA, i) for i in range(NA)])


def gather_y(x):
    return [x] + [from_y(x, r) for r in range(1, NA)]


def swap(x, axis):
    return lax.ppermute(x, axis, [(0, 1), (1, 0)])


def place():
    return lax.axis_index("y"), lax.axis_index("z"), lax.axis_index("xl")


def head_place():
    return lax.axis_index("xh"), lax.axis_index("core")


def per_device(queries, keys, values, evict_logits, block_order, grad_y, w_out):
    plan = run_plan(place, block_order)
    keys, plan = lax.optimization_barrier((keys, plan))
    kv = lax.all_to_all(run_pack(keys, values, evict_logits), "z", 0, 0, tiled=True)
    over = swap(grad_y, "xh")
    pieces = (grad_y, over, swap(grad_y, "core"), swap(over, "core"))
    q_all = gather_y(queries)
    cot = run_cotangent(head_place, pieces, w_out)
    kv_other = swap(kv, "xl")
    cot_all = gather_y(cot)
    sums0, exps0, (qs, qt) = run_forward(0, plan, q_all, kv)
    sums1, exps1, _ = run_forward(1, plan, (qt,), kv_other)
    stats, cs, ct = run_weigh((*sums0, *sums1), cot_all)
    rows = (qs, cs, ct)
    stats = gather_y(stats)
    dq_sum, dkv_other = run_backward(1, plan, rows, kv_other, exps1, stats)
    dkv_here = swap(dkv_other, "xl")
    *dq, dkv = run_backward(0, plan, rows, kv, exps0, stats, dq_sum)
    dkv = (dkv + dkv_here.astype(f32)).astype(bf16)
    dkv = lax.all_to_all(dkv, "z", 0, 0, tiled=True)
    key_grad, value_grad, logit_grad = run_total(dkv, evict_logits)
    query_grad = dq[0].astype(f32)
    for r in range(1, NA):
        query_grad = query_grad + from_y(dq[r], NA - r).astype(f32)
    return query_grad.astype(bf16), key_grad, value_grad, logit_grad


def solution(mesh):
    split = Mesh(mesh.devices.reshape(4, 8, 2, 2, 2), ("y", "z", "xl", "xh", "core"))
    ctx, head = ("y", "z", "xl"), ("xh", "core")
    return jax.shard_map(
        per_device,
        mesh=split,
        in_specs=(
            P(head, ctx, None),
            P(head, ctx, None),
            P(head, ctx, None),
            P(head, ctx),
            P(),
            P(ctx + head, None),
            P(head, None),
        ),
        out_specs=(
            P(head, ctx, None),
            P(head, ctx, None),
            P(head, ctx, None),
            P(head, ctx),
        ),
        check_vma=False,
    )
```

```python
import functools
import math

import jax
import jax.numpy as jnp
from jax import lax
from jax.experimental import pallas as pl
from jax.experimental.pallas import tpu as pltpu
from jax.sharding import Mesh, PartitionSpec as P

WINDOW = 256
HD = 128
HALF = 64
SHARD = 128
HEADS = 8
ROWS = HEADS * HALF
BLOCKS = 128
LOWEST = -1e30
SCALE = 1.0 / math.sqrt(HD)

NA = 4
NZ = 8
SLOTS = 2 * NZ
QB = 2 * NA
KV_ROWS = 2 * SHARD + 16

FULL, PART = 4, 2
CK = FULL * HALF
PER_BLOCK = SLOTS // FULL
UNITS = SLOTS // PART
TILES = [slice(j * SHARD, (j + 1) * SHARD) for j in range(ROWS // SHARD)]
WIDE = 256
WIDE_TILES = [slice(j * WIDE, (j + 1) * WIDE) for j in range(ROWS // WIDE)]
SKIP = 64
HIDDEN = 1000

QBLOCK_AT, SEEN_AT, SLOT_AT, POS_AT = 0, 1, 3, 5

NT = (((1,), (1,)), ((), ()))
NN = (((1,), (0,)), ((), ()))
f32, bf16, i32 = jnp.float32, jnp.bfloat16, jnp.int32


def dot(a, b, dims):
    return lax.dot_general(a, b, dims, preferred_element_type=f32)


def plan_of(blocks, y, z, xl):
    shape = (8, NA * NZ * 2)
    sub = lax.broadcasted_iota(i32, shape, 0)
    lane = lax.broadcasted_iota(i32, shape, 1)
    low = jnp.broadcast_to(blocks[0:1, :].astype(f32), shape)
    high = BLOCKS - 1.0 - low

    def picked(mask, value, axis=1):
        return jnp.sum(jnp.where(mask, value, 0.0), axis=axis, keepdims=True)

    q_low = picked(lane == ((y + (sub >> 1)) & (NA - 1)) * (2 * NZ) + z * 2 + xl, low)
    q_block = jnp.where((sub[:, :1] & 1) == 1, BLOCKS - 1.0 - q_low, q_low)
    columns = {QBLOCK_AT: q_block}
    for col in range(2):
        x = xl if col == 0 else 1 - xl
        here = ((lane >> 4) == y) & ((lane & 1) == x)
        columns[SEEN_AT + col] = picked(here & (low <= q_block), 1.0) + picked(here & (high <= q_block), 1.0)
        k_low = picked(here & (((lane >> 1) & (NZ - 1)) == sub), low)
        columns[SLOT_AT + col] = picked(here & (low < k_low), 1.0)
        rank = picked(k_low < low, 1.0, axis=0)
        columns[POS_AT + col] = picked(here & (rank == sub.astype(f32)), low)
    at = lax.broadcasted_iota(i32, (8, SHARD), 1)
    return sum(jnp.where(at == n, value, 0.0) for n, value in columns.items()).astype(i32)


def pack_kernel(where, k_ref, v_ref, logit_ref, blocks_ref, out_ref, plan_ref):
    plan_ref[...] = plan_of(blocks_ref[...], *where())
    logit = logit_ref[...]
    penalty = jnp.maximum(logit, 0.0) + jnp.log(1.0 + jnp.exp(-jnp.abs(logit)))
    upper = penalty.astype(bf16).astype(f32)
    tail = jnp.concatenate([upper, penalty - upper, jnp.zeros((14, SHARD), f32)], axis=0).astype(bf16)
    for j in range(NZ):
        out_ref[j, 0:SHARD, :] = k_ref[0]
        out_ref[j, SHARD : 2 * SHARD, :] = v_ref[0]
        out_ref[j, 2 * SHARD :, :] = tail


def cotangent_kernel(where, g0, g1, g2, g3, w_hbm, out_ref, rows, w_all, sems):
    def fetch(h):
        here = slice(h * HD, (h + 1) * HD)
        return pltpu.make_async_copy(w_hbm.at[here, :], w_all.at[here, :], sems.at[h])

    for h in range(3):
        fetch(h).start()
    xh, core = where()
    pieces = ((xh, core, g0), (1 - xh, core, g1), (xh, 1 - core, g2), (1 - xh, 1 - core, g3))
    for a, b, ref in pieces:
        rows[pl.ds(pl.multiple_of((a * 2 + b) * 32, 32), 32), :] = ref[...]
    for h in range(HEADS):
        fetch(h).wait()
        if h + 3 < HEADS:
            fetch(h + 3).start()
        if h % 2 == 1:
            cot = dot(rows[...], w_all[(h - 1) * HD : (h + 1) * HD, :], NT).astype(bf16)
            out_ref[h - 1] = cot[:, :HD]
            out_ref[h] = cot[:, HD:]


def sort_keys(plan_ref, col, kv_ref, ks, vs, pen=None):
    for j in range(NZ):
        low = plan_ref[j, SLOT_AT + col]
        if pen is not None:
            rows = kv_ref[j, 2 * SHARD : 2 * SHARD + 16, :].astype(f32)
            penalty = jnp.broadcast_to(rows[0:1] + rows[1:2], (SHARD, SHARD)).T
        for half, slot in ((0, low), (1, SLOTS - 1 - low)):
            at = pl.ds(pl.multiple_of(slot * HALF, HALF), HALF)
            here = slice(half * HALF, (half + 1) * HALF)
            ks[at, :] = kv_ref[j, here, :]
            vs[at, :] = kv_ref[j, SHARD + half * HALF : SHARD + (half + 1) * HALF, :]
            if pen is not None:
                pen[at, :] = penalty[here, :]


def turn(src, dest):
    for i in range(SLOTS * HALF // SHARD):
        dest[i] = src[i * SHARD : (i + 1) * SHARD, :].astype(f32).T.astype(bf16)


def list_steps(plan_ref, col, pos, steps, parts):
    for n in range(NZ):
        low = plan_ref[n, POS_AT + col]
        pos[n] = low
        pos[SLOTS - 1 - n] = BLOCKS - 1 - low
    n_full = jnp.int32(0)
    n_part = jnp.int32(2)
    for rh in range(QB):
        units = (plan_ref[rh, SEEN_AT + col] + PART - 1) // PART
        groups = units // 2
        for c in range(PER_BLOCK):
            steps[n_full] = rh * PER_BLOCK + c
            n_full = n_full + (c < groups).astype(i32)
        parts[n_part] = rh * UNITS + units - 1
        n_part = n_part + (units - 2 * groups)
    last = steps[n_full - 1]
    unit = (last // PER_BLOCK) * UNITS + 2 * (last % PER_BLOCK)
    parts[0] = unit
    parts[1] = unit + 1
    odd = lax.rem(n_full, 2)
    n_full = n_full - odd
    from_part = 2 - 2 * odd
    parts[n_part] = parts[n_part - 1] + SKIP
    for i in range(2):
        steps[n_full + i] = last
        parts[n_part + 1 + i] = parts[n_part]
    n_part = n_part - from_part
    return n_full, n_part + lax.rem(n_part, 2), from_part


def step_of(lists, size, t):
    steps, parts, n_full, from_part = lists
    if size == FULL:
        v = steps[t]
        return v, (v // PER_BLOCK) % QB, (v % PER_BLOCK) * FULL, 2 * t
    v = parts[from_part + t]
    return v, (v // UNITS) % QB, (v % UNITS) * PART, 2 * n_full + t


def rows_at(first, size):
    return pl.ds(pl.multiple_of(first * HALF, SHARD), size * HALF)


def thresholds(plan_ref, pos, v, rh, first, size):
    q_block = plan_ref[rh, QBLOCK_AT]
    ahead = [(q_block - pos[first + i]) * HALF for i in range(size)]
    return [(jnp.where(v >= SKIP, HIDDEN, -d), WINDOW - d) for d in ahead]


def offsets():
    shape = (HALF, SHARD)
    return lax.broadcasted_iota(i32, shape, 1) % HALF - lax.broadcasted_iota(i32, shape, 0)


def block_rows(first, i):
    return pl.ds(pl.multiple_of((first + i) * HALF, HALF), HALF)


def turned_piece(ref, first, size):
    n = size // PART
    return jnp.concatenate([ref[first // PART + i] for i in range(n)], axis=1)


def load_rows(refs, dest):
    for r, ref in enumerate(refs):
        for half in range(2):
            dest[2 * r + half] = ref[:, half * HALF : (half + 1) * HALF, :].reshape(ROWS, HD)


def forward_kernel(col, plan_ref, *refs):
    if col == 0:
        rows_in, (kv_ref, o_ref, st_ref, peaks, exps, qs, qt), refs = refs[:4], refs[4:11], refs[11:]
    else:
        (qt, kv_ref, o_ref, st_ref, peaks, exps), refs = refs[:6], refs[6:]
    ks, vs, vt, pen, s_a, s_b, f_a, f_b, pos, steps, parts = refs
    n_full, n_part, from_part = list_steps(plan_ref, col, pos, steps, parts)
    lists = (steps, parts, n_full, from_part)
    if col == 0:
        load_rows(rows_in, qs)
        for rh in range(QB):
            qt[rh] = qs[rh].astype(f32).T.astype(bf16)
    sort_keys(plan_ref, col, kv_ref, ks, vs, pen)
    turn(vs, vt)
    o_ref[...] = jnp.zeros_like(o_ref)
    for rh in range(QB):
        st_ref[rh, 0:1, :] = jnp.full((1, ROWS), LOWEST, f32)
        st_ref[rh, 1:2, :] = jnp.zeros((1, ROWS), f32)
    def score(size, t, s_ref):
        _, rh, first, _ = step_of(lists, size, t)
        s_ref[: size * HALF, :] = dot(ks[rows_at(first, size), :], qt[rh], NN)

    def soften(size, t, s_ref, f_ref):
        v, rh, first, unit = step_of(lists, size, t)
        limits = thresholds(plan_ref, pos, v, rh, first, size)
        offset = offsets()
        for lanes in TILES:
            tiles = []
            for i, (seen, late) in enumerate(limits):
                s = s_ref[i * HALF : (i + 1) * HALF, lanes] * SCALE
                s = s - jnp.where(offset >= late, pen[block_rows(first, i), :], 0.0)
                tiles.append(jnp.where(offset >= seen, s, LOWEST))
            peak = st_ref[rh, 0:1, lanes]
            tops = functools.reduce(jnp.maximum, tiles)
            new_peak = jnp.maximum(peak, jnp.max(tops, axis=0, keepdims=True))
            factor = jnp.exp(peak - new_peak)
            tiles = [jnp.exp(s - new_peak) for s in tiles]
            total = jnp.sum(sum(tiles), axis=0, keepdims=True)
            for i, p in enumerate(tiles):
                here = slice((i % PART) * HALF, (i % PART + 1) * HALF)
                exps[unit + i // PART, here, lanes] = p.astype(bf16)
            f_ref[0:1, lanes] = factor
            peaks[unit, 0:1, lanes] = new_peak
            st_ref[rh, 0:1, lanes] = new_peak
            st_ref[rh, 1:2, lanes] = st_ref[rh, 1:2, lanes] * factor + total

    def attend(size, t, f_ref):
        _, rh, first, unit = step_of(lists, size, t)
        p = exps[pl.ds(unit, size // PART)].reshape(size * HALF, ROWS)
        o_ref[rh] = o_ref[rh] * f_ref[0:1, :] + dot(turned_piece(vt, first, size), p, NN)

    def run(size, count):
        start = 0 if size == FULL else 2 * n_full
        exps[pl.ds(start, size // PART)] = jnp.zeros((size // PART, PART * HALF, ROWS), bf16)
        f_b[...] = jnp.ones_like(f_b)
        score(size, 0, s_a)

        def pair(i, _):
            t = 2 * i
            attend(size, jnp.maximum(t - 1, 0), f_b)
            score(size, t + 1, s_b)
            soften(size, t, s_a, f_a)
            attend(size, t, f_a)
            score(size, t + 2, s_a)
            soften(size, t + 1, s_b, f_b)
            return 0

        lax.fori_loop(0, count // 2, pair, 0)
        attend(size, count - 1, f_b)

    run(FULL, n_full)

    @pl.when(n_part > 0)
    def _():
        run(PART, n_part)


def weigh_kernel(o0, st0, o1, st1, c0, c1, c2, c3, out_ref, cs, ct):
    for r, ref in enumerate((c0, c1, c2, c3)):
        for half in range(2):
            rh = 2 * r + half
            rows = ref[:, half * HALF : (half + 1) * HALF, :].reshape(ROWS, HD)
            cot = rows.astype(f32).T
            cs[rh] = rows
            ct[rh] = cot.astype(bf16)
            peak = jnp.maximum(st0[rh, 0:1, :], st1[rh, 0:1, :])
            f0, f1 = (jnp.exp(st[rh, 0:1, :] - peak) for st in (st0, st1))
            total = st0[rh, 1:2, :] * f0 + st1[rh, 1:2, :] * f1
            seen = total > 0.0
            weighted = jnp.sum(cot * (o0[rh] * f0 + o1[rh] * f1), axis=0, keepdims=True)
            safe = jnp.where(seen, total, 1.0)
            out_ref[rh : rh + 1, :] = jnp.where(seen, peak + jnp.log(safe), LOWEST)
            out_ref[QB + rh : QB + rh + 1, :] = weighted / safe


def merge_stats(pieces, stats):
    for r in range(NA):
        for half in range(2):
            rh = 2 * r + half
            parts = [(ref, 2 * ((r - t) % NA) + half) for t, ref in enumerate(pieces)]
            norms = [ref[n : n + 1, :] for ref, n in parts]
            means = [ref[QB + n : QB + n + 1, :] for ref, n in parts]
            peak = functools.reduce(jnp.maximum, norms)
            shares = [jnp.exp(norm - peak) for norm in norms]
            total = sum(shares)
            stats[rh, 0:1, :] = peak + jnp.log(total)
            stats[rh, 1:2, :] = sum(share * mean for share, mean in zip(shares, means)) / total


def backward_kernel(col, plan_ref, *refs):
    (qs, cs, ct, kv_ref, peaks, exps), pieces, refs = refs[:6], refs[6:10], refs[10:]
    if col == 1:
        (dq, dkv_ref), refs = refs[:2], refs[2:]
    else:
        (dq_before,), dq_out, (dkv_ref,), refs = refs[:1], refs[1:5], refs[5:6], refs[6:]
        (dq, turned, sems), refs = refs[:3], refs[3:]
    ks, vs, kt, dk, dv, dl, stats, p_a, p_b, d_a, d_b, pos, steps, parts = refs
    n_full, n_part, from_part = list_steps(plan_ref, col, pos, steps, parts)
    lists = (steps, parts, n_full, from_part)
    sort_keys(plan_ref, col, kv_ref, ks, vs)
    turn(ks, kt)
    for ref in (dk, dv, dl):
        ref[...] = jnp.zeros_like(ref)
    dq[...] = jnp.zeros_like(dq) if col == 1 else dq_before[...]
    merge_stats(pieces, stats)

    def differ(size, t, p_ref, d_ref):
        v, rh, first, unit = step_of(lists, size, t)
        offset = offsets()
        limits = thresholds(plan_ref, pos, v, rh, first, size)
        shares = [jnp.exp(peaks[unit, 0:1, lanes] - stats[rh, 0:1, lanes]) for lanes in TILES]
        for half in range(size // PART):
            blocks = range(half * PART, (half + 1) * PART)
            late_sums = [dl[block_rows(first, i), :] for i in blocks]
            at = rows_at(first + half * PART, PART)
            for wide in WIDE_TILES:
                grad = dot(vs[at, :], ct[rh, :, wide], NN)
                for n, i in enumerate(blocks):
                    rows = slice(i * HALF, (i + 1) * HALF)
                    inner = slice(n * HALF, (n + 1) * HALF)
                    for j in range(WIDE // SHARD):
                        here = slice(j * SHARD, (j + 1) * SHARD)
                        lanes = slice(wide.start + here.start, wide.start + here.stop)
                        p = exps[unit + half, inner, lanes].astype(f32) * shares[lanes.start // SHARD]
                        d = p * (grad[inner, here] - stats[rh, 1:2, lanes])
                        late_sums[n] = late_sums[n] + jnp.where(offset >= limits[i][1], d, 0.0)
                        p_ref[rows, lanes] = p.astype(bf16)
                        d_ref[rows, lanes] = d.astype(bf16)
            for n, i in enumerate(blocks):
                dl[block_rows(first, i), :] = late_sums[n]

    def gather(size, t, p_ref, d_ref):
        _, rh, first, _ = step_of(lists, size, t)
        at, rows = rows_at(first, size), size * HALF
        dk[at, :] += dot(d_ref[:rows, :], qs[rh], NN)
        dv[at, :] += dot(p_ref[:rows, :], cs[rh], NN)
        dq[rh] += dot(turned_piece(kt, first, size), d_ref[:rows, :], NN)

    def run(size, count):
        for ref in (p_b, d_b):
            ref[...] = jnp.zeros_like(ref)

        def pair(i, _):
            t = 2 * i
            gather(size, jnp.maximum(t - 1, 0), p_b, d_b)
            differ(size, t, p_a, d_a)
            gather(size, t, p_a, d_a)
            differ(size, t + 1, p_b, d_b)
            return 0

        lax.fori_loop(0, count // 2, pair, 0)
        gather(size, count - 1, p_b, d_b)

    run(FULL, n_full)

    @pl.when(n_part > 0)
    def _():
        run(PART, n_part)

    copies = []
    if col == 0:
        for r, ref in enumerate(dq_out):
            for half in range(2):
                rows = (dq[2 * r + half].T * SCALE).astype(bf16)
                turned[r, :, half * HALF : (half + 1) * HALF, :] = rows.reshape(HEADS, HALF, HD)
            copies.append(pltpu.make_async_copy(turned.at[r], ref, sems.at[r]))
            copies[-1].start()
    for j in range(NZ):
        low = plan_ref[j, SLOT_AT + col]
        spots = [pl.ds(pl.multiple_of(slot * HALF, HALF), HALF) for slot in (low, SLOTS - 1 - low)]
        for half, at in enumerate(spots):
            dkv_ref[j, half * HALF : (half + 1) * HALF, :] = (dk[at, :] * SCALE).astype(dkv_ref.dtype)
            dkv_ref[j, SHARD + half * HALF : SHARD + (half + 1) * HALF, :] = dv[at, :].astype(dkv_ref.dtype)
        late = jnp.concatenate([dl[at, :] for at in spots], axis=0)
        total = jnp.sum(late.T, axis=0, keepdims=True)
        dkv_ref[j, 2 * SHARD : 2 * SHARD + 16, :] = jnp.concatenate(
            [total, jnp.zeros((15, SHARD), f32)], axis=0
        ).astype(dkv_ref.dtype)
    for copy in copies:
        copy.wait()


def total_kernel(parts_ref, logit_ref, dk_ref, dv_ref, dl_ref):
    total = parts_ref[0].astype(f32)
    for n in range(1, NZ):
        total = total + parts_ref[n].astype(f32)
    dk_ref[0] = total[:SHARD]
    dv_ref[0] = total[SHARD : 2 * SHARD]
    dl_ref[...] = -jax.nn.sigmoid(logit_ref[...]) * total[2 * SHARD : 2 * SHARD + 1]


VMEM = pl.BlockSpec(memory_space=pltpu.VMEM)
SMEM = pl.BlockSpec(memory_space=pltpu.SMEM)
HBM = pl.BlockSpec(memory_space=pltpu.HBM)


def grant(mib):
    return pltpu.CompilerParams(vmem_limit_bytes=mib * 1024 * 1024)


MOST = 9 * NA
KEYS = SLOTS * HALF
shaped = jax.ShapeDtypeStruct


def cost(us):
    return pl.CostEstimate(flops=int(us * 1e9), bytes_accessed=2**20, transcendentals=0)


def run_pack(where, keys, values, logits, block_order):
    return pl.pallas_call(
        functools.partial(pack_kernel, where),
        out_shape=(shaped((NZ, KV_ROWS, HD), bf16), shaped((8, SHARD), i32)),
        in_specs=[VMEM] * 4,
        out_specs=(VMEM, VMEM),
        name="pack",
    )(keys, values, logits, block_order.T)


def run_cotangent(where, pieces, w_out):
    return pl.pallas_call(
        functools.partial(cotangent_kernel, where),
        out_shape=shaped((HEADS, SHARD, HD), bf16),
        in_specs=[VMEM] * 4 + [pl.BlockSpec(memory_space=pl.ANY)],
        out_specs=VMEM,
        scratch_shapes=[
            pltpu.VMEM((SHARD, w_out.shape[1]), bf16),
            pltpu.VMEM(w_out.shape, bf16),
            pltpu.SemaphoreType.DMA((HEADS,)),
        ],
        compiler_params=grant(52),
        cost_estimate=cost(5),
        name="cotangent",
    )(*pieces, w_out)


def run_forward(col, plan, q, kv):
    out_shape = (
        shaped((QB, HD, ROWS), f32),
        shaped((QB, 2, ROWS), f32),
        shaped((MOST, 1, ROWS), f32),
        shaped((MOST, PART * HALF, ROWS), bf16),
    )
    if col == 0:
        out_shape += (shaped((QB, ROWS, HD), bf16), shaped((QB, HD, ROWS), bf16))
    o, st, peaks, exps, *turned = pl.pallas_call(
        functools.partial(forward_kernel, col),
        out_shape=out_shape,
        in_specs=[SMEM] + [VMEM] * (len(q) + 1),
        out_specs=(VMEM,) * len(out_shape),
        scratch_shapes=[
            pltpu.VMEM((KEYS, HD), bf16),
            pltpu.VMEM((KEYS, HD), bf16),
            pltpu.VMEM((KEYS // SHARD, HD, SHARD), bf16),
            pltpu.VMEM((KEYS, SHARD), f32),
            pltpu.VMEM((CK, ROWS), f32),
            pltpu.VMEM((CK, ROWS), f32),
            pltpu.VMEM((8, ROWS), f32),
            pltpu.VMEM((8, ROWS), f32),
            pltpu.SMEM((SLOTS,), i32),
            pltpu.SMEM((QB * PER_BLOCK + 3,), i32),
            pltpu.SMEM((2 + QB + 3,), i32),
        ],
        compiler_params=grant(14),
        cost_estimate=cost(10),
        name=f"forward{col}",
    )(plan, *q, kv)
    return (o, st), (peaks, exps), turned


def run_weigh(sums, cot):
    return pl.pallas_call(
        weigh_kernel,
        out_shape=(
            shaped((2 * QB, ROWS), f32),
            shaped((QB, ROWS, HD), bf16),
            shaped((QB, HD, ROWS), bf16),
        ),
        in_specs=[VMEM] * 8,
        out_specs=(VMEM,) * 3,
        compiler_params=grant(8),
        name="weigh",
    )(*sums, *cot)


def run_backward(col, plan, rows, kv, exps, stats, dq_sum=None):
    if col == 1:
        more, scratch = (), []
        out_shape = (shaped((QB, HD, ROWS), f32), shaped((NZ, KV_ROWS, HD), bf16))
        out_specs = (VMEM, VMEM)
    else:
        more = (dq_sum,)
        scratch = [
            pltpu.VMEM((QB, HD, ROWS), f32),
            pltpu.VMEM((NA, HEADS, SHARD, HD), bf16),
            pltpu.SemaphoreType.DMA((NA,)),
        ]
        out_shape = (shaped((HEADS, SHARD, HD), bf16),) * NA + (shaped((NZ, KV_ROWS, HD), f32),)
        out_specs = (HBM,) * NA + (VMEM,)
    return pl.pallas_call(
        functools.partial(backward_kernel, col),
        out_shape=out_shape,
        in_specs=[SMEM] + [VMEM] * (10 + len(more)),
        out_specs=out_specs,
        scratch_shapes=scratch
        + [
            pltpu.VMEM((KEYS, HD), bf16),
            pltpu.VMEM((KEYS, HD), bf16),
            pltpu.VMEM((KEYS // SHARD, HD, SHARD), bf16),
            pltpu.VMEM((KEYS, HD), f32),
            pltpu.VMEM((KEYS, HD), f32),
            pltpu.VMEM((KEYS, SHARD), f32),
            pltpu.VMEM((QB, 2, ROWS), f32),
        ]
        + [pltpu.VMEM((CK, ROWS), bf16)] * 4
        + [pltpu.SMEM((SLOTS,), i32), pltpu.SMEM((QB * PER_BLOCK + 3,), i32), pltpu.SMEM((2 + QB + 3,), i32)],
        compiler_params=grant(18),
        cost_estimate=cost(15),
        name=f"backward{col}",
    )(plan, *rows, kv, *exps, *stats, *more)


def run_total(parts, logits):
    return pl.pallas_call(
        total_kernel,
        out_shape=(shaped((1, SHARD, HD), f32), shaped((1, SHARD, HD), f32), shaped((1, SHARD), f32)),
        in_specs=[VMEM] * 2,
        out_specs=(VMEM,) * 3,
        compiler_params=grant(4),
        name="total",
    )(parts, logits)


def from_y(x, r):
    return lax.ppermute(x, "y", [((i + r) % NA, i) for i in range(NA)])


def gather_y(x):
    return [x] + [from_y(x, r) for r in range(1, NA)]


def swap(x, axis):
    return lax.ppermute(x, axis, [(0, 1), (1, 0)])


def place():
    return lax.axis_index("y"), lax.axis_index("z"), lax.axis_index("xl")


def head_place():
    return lax.axis_index("xh"), lax.axis_index("core")


def per_device(queries, keys, values, evict_logits, block_order, grad_y, w_out):
    packed, plan = run_pack(place, keys, values, evict_logits, block_order)
    kv = lax.all_to_all(packed, "z", 0, 0, tiled=True)
    over = swap(grad_y, "xh")
    pieces = (grad_y, over, swap(grad_y, "core"), swap(over, "core"))
    q_all = gather_y(queries)
    cot = run_cotangent(head_place, pieces, w_out)
    kv_other = swap(kv, "xl")
    cot_all = gather_y(cot)
    sums0, exps0, (qs, qt) = run_forward(0, plan, q_all, kv)
    sums1, exps1, _ = run_forward(1, plan, (qt,), kv_other)
    stats, cs, ct = run_weigh((*sums0, *sums1), cot_all)
    rows = (qs, cs, ct)
    stats = gather_y(stats)
    dq_sum, dkv_other = run_backward(1, plan, rows, kv_other, exps1, stats)
    dkv_here = swap(dkv_other, "xl")
    *dq, dkv = run_backward(0, plan, rows, kv, exps0, stats, dq_sum)
    dkv = (dkv + dkv_here.astype(f32)).astype(bf16)
    dkv = lax.all_to_all(dkv, "z", 0, 0, tiled=True)
    key_grad, value_grad, logit_grad = run_total(dkv, evict_logits)
    query_grad = dq[0].astype(f32)
    for r in range(1, NA):
        query_grad = query_grad + from_y(dq[r], NA - r).astype(f32)
    return query_grad.astype(bf16), key_grad, value_grad, logit_grad


def solution(mesh):
    split = Mesh(mesh.devices.reshape(4, 8, 2, 2, 2), ("y", "z", "xl", "xh", "core"))
    ctx, head = ("y", "z", "xl"), ("xh", "core")
    return jax.shard_map(
        per_device,
        mesh=split,
        in_specs=(
            P(head, ctx, None),
            P(head, ctx, None),
            P(head, ctx, None),
            P(head, ctx),
            P(),
            P(ctx + head, None),
            P(head, None),
        ),
        out_specs=(
            P(head, ctx, None),
            P(head, ctx, None),
            P(head, ctx, None),
            P(head, ctx),
        ),
        check_vma=False,
    )
```

```python
import functools
import math

import jax
import jax.numpy as jnp
from jax import lax
from jax.experimental import pallas as pl
from jax.experimental.pallas import tpu as pltpu
from jax.sharding import Mesh, PartitionSpec as P

WINDOW = 256
HD = 128
HALF = 64
SHARD = 128
HEADS = 8
ROWS = HEADS * HALF
BLOCKS = 128
LOWEST = -1e30
SCALE = 1.0 / math.sqrt(HD)

NA = 4
NZ = 8
SLOTS = 2 * NZ
QB = 2 * NA
KV_ROWS = 2 * SHARD + 16

STEP = 4
CK = STEP * HALF
PER_BLOCK = SLOTS // STEP
TILES = [slice(j * SHARD, (j + 1) * SHARD) for j in range(ROWS // SHARD)]
WIDE = 256
WIDE_TILES = [slice(j * WIDE, (j + 1) * WIDE) for j in range(ROWS // WIDE)]
STREAMS = (0, 1)
QS = QB // 2
LIST = 24
SKIP = 64
HIDDEN = 1000

QBLOCK_AT, SEEN_AT, SLOT_AT, POS_AT = 0, 1, 3, 5

NT = (((1,), (1,)), ((), ()))
NN = (((1,), (0,)), ((), ()))
f32, bf16, i32 = jnp.float32, jnp.bfloat16, jnp.int32


def dot(a, b, dims):
    return lax.dot_general(a, b, dims, preferred_element_type=f32)


def plan_of(blocks, y, z, xl):
    shape = (8, NA * NZ * 2)
    sub = lax.broadcasted_iota(i32, shape, 0)
    lane = lax.broadcasted_iota(i32, shape, 1)
    low = jnp.broadcast_to(blocks[0:1, :].astype(f32), shape)
    high = BLOCKS - 1.0 - low

    def picked(mask, value, axis=1):
        return jnp.sum(jnp.where(mask, value, 0.0), axis=axis, keepdims=True)

    q_low = picked(lane == ((y + (sub >> 1)) & (NA - 1)) * (2 * NZ) + z * 2 + xl, low)
    q_block = jnp.where((sub[:, :1] & 1) == 1, BLOCKS - 1.0 - q_low, q_low)
    columns = {QBLOCK_AT: q_block}
    for col in range(2):
        x = xl if col == 0 else 1 - xl
        here = ((lane >> 4) == y) & ((lane & 1) == x)
        columns[SEEN_AT + col] = picked(here & (low <= q_block), 1.0) + picked(here & (high <= q_block), 1.0)
        k_low = picked(here & (((lane >> 1) & (NZ - 1)) == sub), low)
        columns[SLOT_AT + col] = picked(here & (low < k_low), 1.0)
        rank = picked(k_low < low, 1.0, axis=0)
        columns[POS_AT + col] = picked(here & (rank == sub.astype(f32)), low)
    at = lax.broadcasted_iota(i32, (8, SHARD), 1)
    return sum(jnp.where(at == n, value, 0.0) for n, value in columns.items()).astype(i32)


def plan_kernel(where, blocks_ref, plan_ref):
    plan_ref[...] = plan_of(blocks_ref[...], *where())


def pack_kernel(k_ref, v_ref, logit_ref, out_ref):
    logit = logit_ref[...]
    penalty = jnp.maximum(logit, 0.0) + jnp.log(1.0 + jnp.exp(-jnp.abs(logit)))
    upper = penalty.astype(bf16).astype(f32)
    tail = jnp.concatenate([upper, penalty - upper, jnp.zeros((14, SHARD), f32)], axis=0).astype(bf16)
    for j in range(NZ):
        out_ref[j, 0:SHARD, :] = k_ref[0]
        out_ref[j, SHARD : 2 * SHARD, :] = v_ref[0]
        out_ref[j, 2 * SHARD :, :] = tail


def cotangent_kernel(where, g0, g1, g2, g3, w_ref, out_ref, rows):
    xh, core = where()
    pieces = ((xh, core, g0), (1 - xh, core, g1), (xh, 1 - core, g2), (1 - xh, 1 - core, g3))
    for a, b, ref in pieces:
        rows[pl.ds(pl.multiple_of((a * 2 + b) * 32, 32), 32), :] = ref[...]
    for i in range(0, HEADS, 2):
        cot = dot(rows[...], w_ref[i * HD : (i + 2) * HD, :], NT).astype(bf16)
        out_ref[i] = cot[:, :HD]
        out_ref[i + 1] = cot[:, HD:]


def sort_keys(plan_ref, col, kv_ref, ks, vs, pen=None):
    for j in range(NZ):
        low = plan_ref[j, SLOT_AT + col]
        if pen is not None:
            rows = kv_ref[j, 2 * SHARD : 2 * SHARD + 16, :].astype(f32)
            penalty = jnp.broadcast_to(rows[0:1] + rows[1:2], (SHARD, SHARD)).T
        for half, slot in ((0, low), (1, SLOTS - 1 - low)):
            at = pl.ds(pl.multiple_of(slot * HALF, HALF), HALF)
            here = slice(half * HALF, (half + 1) * HALF)
            ks[at, :] = kv_ref[j, here, :]
            vs[at, :] = kv_ref[j, SHARD + half * HALF : SHARD + (half + 1) * HALF, :]
            if pen is not None:
                pen[at, :] = penalty[here, :]


def turn(src, dest):
    for i in range(SLOTS * HALF // SHARD):
        dest[i] = src[i * SHARD : (i + 1) * SHARD, :].astype(f32).T.astype(bf16)


def list_steps(plan_ref, col, pos, steps):
    for n in range(NZ):
        low = plan_ref[n, POS_AT + col]
        pos[n] = low
        pos[SLOTS - 1 - n] = BLOCKS - 1 - low
    counts = []
    for stream in STREAMS:
        count = jnp.int32(0)
        for rh in range(stream * QS, (stream + 1) * QS):
            groups = (plan_ref[rh, SEEN_AT + col] + STEP - 1) // STEP
            for c in range(PER_BLOCK):
                steps[stream * LIST + count] = rh * PER_BLOCK + c
                count = count + (c < groups).astype(i32)
        last = steps[stream * LIST + count - 1]
        for i in range(5):
            steps[stream * LIST + count + i] = last + SKIP
        counts.append(count)
    count = jnp.maximum(*counts)
    return count + lax.rem(count, 2)


def step_of(steps, stream, t):
    v = steps[stream * LIST + t]
    rh = (v // PER_BLOCK) % QB
    c = v % PER_BLOCK
    return v, rh, c, pl.ds(pl.multiple_of(c * CK, CK), CK)


def thresholds(plan_ref, pos, v, rh, c):
    q_block = plan_ref[rh, QBLOCK_AT]
    ahead = [(q_block - pos[c * STEP + i]) * HALF for i in range(STEP)]
    return [(jnp.where(v >= SKIP, HIDDEN, -d), WINDOW - d) for d in ahead]


def offsets():
    shape = (HALF, SHARD)
    return lax.broadcasted_iota(i32, shape, 1) % HALF - lax.broadcasted_iota(i32, shape, 0)


def block_rows(c, i):
    return pl.ds(pl.multiple_of(c * CK + i * HALF, HALF), HALF)


def turned_piece(ref, c):
    n = CK // SHARD
    return jnp.concatenate([ref[c * n + i] for i in range(n)], axis=1)


def load_rows(refs, dest):
    for r, ref in enumerate(refs):
        for half in range(2):
            dest[2 * r + half] = ref[:, half * HALF : (half + 1) * HALF, :].reshape(ROWS, HD)


def forward_kernel(col, plan_ref, *refs):
    if col == 0:
        rows_in, kv_ref, refs = refs[:4], refs[4], refs[5:]
    else:
        (qt, kv_ref), refs = refs[:2], refs[2:]
    os, sts, peaks, exps, refs = refs[:2], refs[2:4], refs[4:6], refs[6:8], refs[8:]
    if col == 0:
        (qs, qt), refs = refs[:2], refs[2:]
    ks, vs, vt, pen, s_0, s_1, s_2, s_3, f_0, f_1, f_2, f_3, pos, steps = refs
    s_even, s_odd, f_even, f_odd = (s_0, s_1), (s_2, s_3), (f_0, f_1), (f_2, f_3)
    count = list_steps(plan_ref, col, pos, steps)
    if col == 0:
        load_rows(rows_in, qs)
        for rh in range(QB):
            qt[rh] = qs[rh].astype(f32).T.astype(bf16)
    sort_keys(plan_ref, col, kv_ref, ks, vs, pen)
    turn(vs, vt)
    for n in STREAMS:
        os[n][...] = jnp.zeros_like(os[n])
        for rh in range(QS):
            sts[n][rh, 0:1, :] = jnp.full((1, ROWS), LOWEST, f32)
            sts[n][rh, 1:2, :] = jnp.zeros((1, ROWS), f32)
        exps[n][0] = jnp.zeros_like(exps[n][0])
        f_odd[n][...] = jnp.ones_like(f_odd[n])

    def score(n, t, s_refs):
        _, rh, _, at = step_of(steps, n, t)
        s_refs[n][...] = dot(ks[at, :], qt[rh], NN)

    def soften(n, t, s_refs, f_refs):
        v, rh, c, _ = step_of(steps, n, t)
        limits = thresholds(plan_ref, pos, v, rh, c)
        offset = offsets()
        st = sts[n]
        rh = rh - n * QS
        for lanes in TILES:
            parts = []
            for i, (seen, late) in enumerate(limits):
                s = s_refs[n][i * HALF : (i + 1) * HALF, lanes] * SCALE
                s = s - jnp.where(offset >= late, pen[block_rows(c, i), :], 0.0)
                parts.append(jnp.where(offset >= seen, s, LOWEST))
            peak = st[rh, 0:1, lanes]
            tops = functools.reduce(jnp.maximum, parts)
            new_peak = jnp.maximum(peak, jnp.max(tops, axis=0, keepdims=True))
            factor = jnp.exp(peak - new_peak)
            parts = [jnp.exp(s - new_peak) for s in parts]
            total = jnp.sum(sum(parts), axis=0, keepdims=True)
            for i, p in enumerate(parts):
                exps[n][t, i * HALF : (i + 1) * HALF, lanes] = p.astype(bf16)
            f_refs[n][0:1, lanes] = factor
            peaks[n][t, 0:1, lanes] = new_peak
            st[rh, 0:1, lanes] = new_peak
            st[rh, 1:2, lanes] = st[rh, 1:2, lanes] * factor + total

    def attend(n, t, f_refs):
        _, rh, c, _ = step_of(steps, n, t)
        rh = rh - n * QS
        os[n][rh] = os[n][rh] * f_refs[n][0:1, :] + dot(turned_piece(vt, c), exps[n][t], NN)

    def both(work, *args):
        for n in STREAMS:
            work(n, *args)

    both(score, 0, s_even)

    def pair(i, _):
        t = 2 * i
        both(attend, jnp.maximum(t - 1, 0), f_odd)
        both(score, t + 1, s_odd)
        both(soften, t, s_even, f_even)
        both(attend, t, f_even)
        both(score, t + 2, s_even)
        both(soften, t + 1, s_odd, f_odd)
        return 0

    lax.fori_loop(0, count // 2, pair, 0)
    both(attend, count - 1, f_odd)


def weigh_kernel(*refs):
    sums, pieces, (out_ref, cs, ct) = (refs[:4], refs[4:8]), refs[8:12], refs[12:]
    for r, ref in enumerate(pieces):
        for half in range(2):
            rh = 2 * r + half
            n, inner = rh // QS, rh % QS
            o0, o1 = (column[n] for column in sums)
            st0, st1 = (column[2 + n] for column in sums)
            rows = ref[:, half * HALF : (half + 1) * HALF, :].reshape(ROWS, HD)
            cot = rows.astype(f32).T
            cs[rh] = rows
            ct[rh] = cot.astype(bf16)
            peak = jnp.maximum(st0[inner, 0:1, :], st1[inner, 0:1, :])
            f0, f1 = (jnp.exp(st[inner, 0:1, :] - peak) for st in (st0, st1))
            total = st0[inner, 1:2, :] * f0 + st1[inner, 1:2, :] * f1
            seen = total > 0.0
            weighted = jnp.sum(cot * (o0[inner] * f0 + o1[inner] * f1), axis=0, keepdims=True)
            safe = jnp.where(seen, total, 1.0)
            out_ref[rh : rh + 1, :] = jnp.where(seen, peak + jnp.log(safe), LOWEST)
            out_ref[QB + rh : QB + rh + 1, :] = weighted / safe


def merge_stats(pieces, stats):
    for r in range(NA):
        for half in range(2):
            rh = 2 * r + half
            parts = [(ref, 2 * ((r - t) % NA) + half) for t, ref in enumerate(pieces)]
            norms = [ref[n : n + 1, :] for ref, n in parts]
            means = [ref[QB + n : QB + n + 1, :] for ref, n in parts]
            peak = functools.reduce(jnp.maximum, norms)
            shares = [jnp.exp(norm - peak) for norm in norms]
            total = sum(shares)
            stats[rh, 0:1, :] = peak + jnp.log(total)
            stats[rh, 1:2, :] = sum(share * mean for share, mean in zip(shares, means)) / total


def backward_kernel(col, plan_ref, *refs):
    (qs, cs, ct, kv_ref), peaks, exps, pieces, refs = refs[:4], refs[4:6], refs[6:8], refs[8:12], refs[12:]
    if col == 1:
        dq, dkv_ref, refs = refs[:2], refs[2], refs[3:]
    else:
        dq_before, dq_out, dkv_ref, dq, refs = refs[:2], refs[2:6], refs[6], refs[7:9], refs[9:]
        (turned, sems), refs = refs[:2], refs[2:]
    (ks, vs, kt, stats), dk, dv, dl, refs = refs[:4], refs[4:6], refs[6:8], refs[8:10], refs[10:]
    p_even, p_odd, d_even, d_odd, (pos, steps) = refs[:2], refs[2:4], refs[4:6], refs[6:8], refs[8:]
    count = list_steps(plan_ref, col, pos, steps)
    sort_keys(plan_ref, col, kv_ref, ks, vs)
    turn(ks, kt)
    for ref in dk + dv + dl + p_odd + d_odd:
        ref[...] = jnp.zeros_like(ref)
    for n in STREAMS:
        dq[n][...] = jnp.zeros_like(dq[n]) if col == 1 else dq_before[n][...]
    merge_stats(pieces, stats)

    def differ(n, t, p_refs, d_refs):
        v, rh, c, _ = step_of(steps, n, t)
        offset = offsets()
        limits = thresholds(plan_ref, pos, v, rh, c)
        shares = [jnp.exp(peaks[n][t, 0:1, lanes] - stats[rh, 0:1, lanes]) for lanes in TILES]
        for first in range(0, STEP, 2):
            blocks = (first, first + 1)
            late_sums = [dl[n][block_rows(c, i), :] for i in blocks]
            at = pl.ds(pl.multiple_of(c * CK + first * HALF, SHARD), 2 * HALF)
            for wide in WIDE_TILES:
                grad = dot(vs[at, :], ct[rh, :, wide], NN)
                for m, i in enumerate(blocks):
                    rows = slice(i * HALF, (i + 1) * HALF)
                    for j in range(WIDE // SHARD):
                        here = slice(j * SHARD, (j + 1) * SHARD)
                        lanes = slice(wide.start + here.start, wide.start + here.stop)
                        p = exps[n][t, rows, lanes].astype(f32) * shares[lanes.start // SHARD]
                        d = p * (grad[m * HALF : (m + 1) * HALF, here] - stats[rh, 1:2, lanes])
                        late_sums[m] = late_sums[m] + jnp.where(offset >= limits[i][1], d, 0.0)
                        p_refs[n][rows, lanes] = p.astype(bf16)
                        d_refs[n][rows, lanes] = d.astype(bf16)
            for m, i in enumerate(blocks):
                dl[n][block_rows(c, i), :] = late_sums[m]

    def gather(n, t, p_refs, d_refs):
        _, rh, c, at = step_of(steps, n, t)
        dk[n][at, :] += dot(d_refs[n][...], qs[rh], NN)
        dv[n][at, :] += dot(p_refs[n][...], cs[rh], NN)
        dq[n][rh - n * QS] += dot(turned_piece(kt, c), d_refs[n][...], NN)

    def both(work, *args):
        for n in STREAMS:
            work(n, *args)

    def pair(i, _):
        t = 2 * i
        both(gather, jnp.maximum(t - 1, 0), p_odd, d_odd)
        both(differ, t, p_even, d_even)
        both(gather, t, p_even, d_even)
        both(differ, t + 1, p_odd, d_odd)
        return 0

    lax.fori_loop(0, count // 2, pair, 0)
    both(gather, count - 1, p_odd, d_odd)
    copies = []
    if col == 0:
        for r, ref in enumerate(dq_out):
            for half in range(2):
                rows = (dq[r // 2][2 * (r % 2) + half].T * SCALE).astype(bf16)
                turned[r, :, half * HALF : (half + 1) * HALF, :] = rows.reshape(HEADS, HALF, HD)
            copies.append(pltpu.make_async_copy(turned.at[r], ref, sems.at[r]))
            copies[-1].start()
    for j in range(NZ):
        low = plan_ref[j, SLOT_AT + col]
        spots = [pl.ds(pl.multiple_of(slot * HALF, HALF), HALF) for slot in (low, SLOTS - 1 - low)]
        for half, at in enumerate(spots):
            key_sum = (dk[0][at, :] + dk[1][at, :]) * SCALE
            value_sum = dv[0][at, :] + dv[1][at, :]
            dkv_ref[j, half * HALF : (half + 1) * HALF, :] = key_sum.astype(dkv_ref.dtype)
            dkv_ref[j, SHARD + half * HALF : SHARD + (half + 1) * HALF, :] = value_sum.astype(dkv_ref.dtype)
        late = jnp.concatenate([dl[0][at, :] + dl[1][at, :] for at in spots], axis=0)
        total = jnp.sum(late.T, axis=0, keepdims=True)
        dkv_ref[j, 2 * SHARD : 2 * SHARD + 16, :] = jnp.concatenate(
            [total, jnp.zeros((15, SHARD), f32)], axis=0
        ).astype(dkv_ref.dtype)
    for copy in copies:
        copy.wait()


def total_kernel(parts_ref, logit_ref, dk_ref, dv_ref, dl_ref):
    total = parts_ref[0].astype(f32)
    for n in range(1, NZ):
        total = total + parts_ref[n].astype(f32)
    dk_ref[0] = total[:SHARD]
    dv_ref[0] = total[SHARD : 2 * SHARD]
    dl_ref[...] = -jax.nn.sigmoid(logit_ref[...]) * total[2 * SHARD : 2 * SHARD + 1]


VMEM = pl.BlockSpec(memory_space=pltpu.VMEM)
SMEM = pl.BlockSpec(memory_space=pltpu.SMEM)
HBM = pl.BlockSpec(memory_space=pltpu.HBM)


def grant(mib):
    return pltpu.CompilerParams(vmem_limit_bytes=mib * 1024 * 1024)


MOST = 5 * NA // 2
KEYS = SLOTS * HALF
shaped = jax.ShapeDtypeStruct


def cost(us):
    return pl.CostEstimate(flops=int(us * 1e9), bytes_accessed=2**20, transcendentals=0)


def run_plan(where, block_order):
    return pl.pallas_call(
        functools.partial(plan_kernel, where),
        out_shape=shaped((8, SHARD), i32),
        in_specs=[VMEM],
        out_specs=VMEM,
        compiler_params=grant(4),
        cost_estimate=cost(12),
        name="plan",
    )(block_order.T)


def run_pack(keys, values, logits):
    return pl.pallas_call(
        pack_kernel,
        out_shape=shaped((NZ, KV_ROWS, HD), bf16),
        in_specs=[VMEM] * 3,
        out_specs=VMEM,
        compiler_params=grant(4),
        name="pack",
    )(keys, values, logits)


def run_cotangent(where, pieces, w_out):
    return pl.pallas_call(
        functools.partial(cotangent_kernel, where),
        out_shape=shaped((HEADS, SHARD, HD), bf16),
        in_specs=[VMEM] * 5,
        out_specs=VMEM,
        scratch_shapes=[pltpu.VMEM((SHARD, w_out.shape[1]), bf16)],
        compiler_params=grant(8),
        cost_estimate=cost(5),
        name="cotangent",
    )(*pieces, w_out)


def run_forward(col, plan, q, kv):
    out_shape = (
        (shaped((QS, HD, ROWS), f32),) * 2
        + (shaped((QS, 2, ROWS), f32),) * 2
        + (shaped((MOST, 1, ROWS), f32),) * 2
        + (shaped((MOST, CK, ROWS), bf16),) * 2
    )
    if col == 0:
        out_shape += (shaped((QB, ROWS, HD), bf16), shaped((QB, HD, ROWS), bf16))
    out = pl.pallas_call(
        functools.partial(forward_kernel, col),
        out_shape=out_shape,
        in_specs=[SMEM] + [VMEM] * (len(q) + 1),
        out_specs=(VMEM,) * len(out_shape),
        scratch_shapes=[
            pltpu.VMEM((KEYS, HD), bf16),
            pltpu.VMEM((KEYS, HD), bf16),
            pltpu.VMEM((KEYS // SHARD, HD, SHARD), bf16),
            pltpu.VMEM((KEYS, SHARD), f32),
        ]
        + [pltpu.VMEM((CK, ROWS), f32)] * 4
        + [pltpu.VMEM((8, ROWS), f32)] * 4
        + [pltpu.SMEM((SLOTS,), i32), pltpu.SMEM((2 * LIST,), i32)],
        compiler_params=grant(16),
        cost_estimate=cost(10),
        name=f"forward{col}",
    )(plan, *q, kv)
    return out[:4], out[4:8], out[8:]


def run_weigh(sums, cot):
    return pl.pallas_call(
        weigh_kernel,
        out_shape=(
            shaped((2 * QB, ROWS), f32),
            shaped((QB, ROWS, HD), bf16),
            shaped((QB, HD, ROWS), bf16),
        ),
        in_specs=[VMEM] * 12,
        out_specs=(VMEM,) * 3,
        compiler_params=grant(8),
        name="weigh",
    )(*sums, *cot)


def run_backward(col, plan, rows, kv, exps, stats, dq_sum=()):
    sums = [pltpu.VMEM((QS, HD, ROWS), f32)] * 2
    if col == 1:
        scratch = []
        out_shape = (shaped((QS, HD, ROWS), f32),) * 2 + (shaped((NZ, KV_ROWS, HD), bf16),)
        out_specs = (VMEM,) * 3
    else:
        scratch = sums + [
            pltpu.VMEM((NA, HEADS, SHARD, HD), bf16),
            pltpu.SemaphoreType.DMA((NA,)),
        ]
        out_shape = (shaped((HEADS, SHARD, HD), bf16),) * NA + (shaped((NZ, KV_ROWS, HD), f32),)
        out_specs = (HBM,) * NA + (VMEM,)
    return pl.pallas_call(
        functools.partial(backward_kernel, col),
        out_shape=out_shape,
        in_specs=[SMEM] + [VMEM] * (12 + len(dq_sum)),
        out_specs=out_specs,
        scratch_shapes=scratch
        + [
            pltpu.VMEM((KEYS, HD), bf16),
            pltpu.VMEM((KEYS, HD), bf16),
            pltpu.VMEM((KEYS // SHARD, HD, SHARD), bf16),
            pltpu.VMEM((QB, 2, ROWS), f32),
        ]
        + [pltpu.VMEM((KEYS, HD), f32)] * 6
        + [pltpu.VMEM((CK, ROWS), bf16)] * 8
        + [pltpu.SMEM((SLOTS,), i32), pltpu.SMEM((2 * LIST,), i32)],
        compiler_params=grant(22),
        cost_estimate=cost(15),
        name=f"backward{col}",
    )(plan, *rows, kv, *exps, *stats, *dq_sum)


def run_total(parts, logits):
    return pl.pallas_call(
        total_kernel,
        out_shape=(shaped((1, SHARD, HD), f32), shaped((1, SHARD, HD), f32), shaped((1, SHARD), f32)),
        in_specs=[VMEM] * 2,
        out_specs=(VMEM,) * 3,
        compiler_params=grant(4),
        name="total",
    )(parts, logits)


def from_y(x, r):
    return lax.ppermute(x, "y", [((i + r) % NA, i) for i in range(NA)])


def gather_y(x):
    return [x] + [from_y(x, r) for r in range(1, NA)]


def swap(x, axis):
    return lax.ppermute(x, axis, [(0, 1), (1, 0)])


def place():
    return lax.axis_index("y"), lax.axis_index("z"), lax.axis_index("xl")


def head_place():
    return lax.axis_index("xh"), lax.axis_index("core")


def per_device(queries, keys, values, evict_logits, block_order, grad_y, w_out):
    plan = run_plan(place, block_order)
    keys, plan = lax.optimization_barrier((keys, plan))
    kv = lax.all_to_all(run_pack(keys, values, evict_logits), "z", 0, 0, tiled=True)
    over = swap(grad_y, "xh")
    pieces = (grad_y, over, swap(grad_y, "core"), swap(over, "core"))
    q_all = gather_y(queries)
    cot = run_cotangent(head_place, pieces, w_out)
    kv_other = swap(kv, "xl")
    cot_all = gather_y(cot)
    sums0, exps0, (qs, qt) = run_forward(0, plan, q_all, kv)
    sums1, exps1, _ = run_forward(1, plan, (qt,), kv_other)
    stats, cs, ct = run_weigh((*sums0, *sums1), cot_all)
    rows = (qs, cs, ct)
    stats = gather_y(stats)
    *dq_sum, dkv_other = run_backward(1, plan, rows, kv_other, exps1, stats)
    dkv_here = swap(dkv_other, "xl")
    *dq, dkv = run_backward(0, plan, rows, kv, exps0, stats, dq_sum)
    dkv = (dkv + dkv_here.astype(f32)).astype(bf16)
    dkv = lax.all_to_all(dkv, "z", 0, 0, tiled=True)
    key_grad, value_grad, logit_grad = run_total(dkv, evict_logits)
    query_grad = dq[0].astype(f32)
    for r in range(1, NA):
        query_grad = query_grad + from_y(dq[r], NA - r).astype(f32)
    return query_grad.astype(bf16), key_grad, value_grad, logit_grad


def solution(mesh):
    split = Mesh(mesh.devices.reshape(4, 8, 2, 2, 2), ("y", "z", "xl", "xh", "core"))
    ctx, head = ("y", "z", "xl"), ("xh", "core")
    return jax.shard_map(
        per_device,
        mesh=split,
        in_specs=(
            P(head, ctx, None),
            P(head, ctx, None),
            P(head, ctx, None),
            P(head, ctx),
            P(),
            P(ctx + head, None),
            P(head, None),
        ),
        out_specs=(
            P(head, ctx, None),
            P(head, ctx, None),
            P(head, ctx, None),
            P(head, ctx),
        ),
        check_vma=False,
    )
```

```python
import functools
import math

import jax
import jax.numpy as jnp
from jax import lax
from jax.experimental import pallas as pl
from jax.experimental.pallas import tpu as pltpu
from jax.sharding import Mesh, PartitionSpec as P

WINDOW = 256
HD = 128
HALF = 64
SHARD = 128
HEADS = 8
ROWS = HEADS * HALF
BLOCKS = 128
LOWEST = -1e30
SCALE = 1.0 / math.sqrt(HD)

NA = 4
NZ = 8
SLOTS = 2 * NZ
QB = 2 * NA
KV_ROWS = 2 * SHARD + 16

STEP = 4
CK = STEP * HALF
PER_BLOCK = SLOTS // STEP
TILES = [slice(j * SHARD, (j + 1) * SHARD) for j in range(ROWS // SHARD)]
WIDE = 256
WIDE_TILES = [slice(j * WIDE, (j + 1) * WIDE) for j in range(ROWS // WIDE)]
STREAMS = (0, 1)
QS = QB // 2
LIST = 24
COUNT_AT, KEPT_AT, LISTED_AT, LISTS = 2 * LIST, 64, 128, 256
SKIP = 64
HIDDEN = 1000

QBLOCK_AT, SEEN_AT, SLOT_AT, POS_AT, FAR_AT = 0, 1, 3, 5, 7
FAR = (WINDOW + 2 * HALF - 2) // HALF

NT = (((1,), (1,)), ((), ()))
NN = (((1,), (0,)), ((), ()))
f32, bf16, i32 = jnp.float32, jnp.bfloat16, jnp.int32


def dot(a, b, dims):
    return lax.dot_general(a, b, dims, preferred_element_type=f32)


def plan_of(blocks, y, z, xl):
    shape = (8, NA * NZ * 2)
    sub = lax.broadcasted_iota(i32, shape, 0)
    lane = lax.broadcasted_iota(i32, shape, 1)
    low = jnp.broadcast_to(blocks[0:1, :].astype(f32), shape)
    high = BLOCKS - 1.0 - low

    def picked(mask, value, axis=1):
        return jnp.sum(jnp.where(mask, value, 0.0), axis=axis, keepdims=True)

    q_low = picked(lane == ((y + (sub >> 1)) & (NA - 1)) * (2 * NZ) + z * 2 + xl, low)
    q_block = jnp.where((sub[:, :1] & 1) == 1, BLOCKS - 1.0 - q_low, q_low)
    columns = {QBLOCK_AT: q_block}
    for col in range(2):
        x = xl if col == 0 else 1 - xl
        here = ((lane >> 4) == y) & ((lane & 1) == x)
        columns[SEEN_AT + col] = picked(here & (low <= q_block), 1.0) + picked(here & (high <= q_block), 1.0)
        far = q_block - FAR
        columns[FAR_AT + col] = picked(here & (low <= far), 1.0) + picked(here & (high <= far), 1.0)
        k_low = picked(here & (((lane >> 1) & (NZ - 1)) == sub), low)
        columns[SLOT_AT + col] = picked(here & (low < k_low), 1.0)
        rank = picked(k_low < low, 1.0, axis=0)
        columns[POS_AT + col] = picked(here & (rank == sub.astype(f32)), low)
    at = lax.broadcasted_iota(i32, (8, SHARD), 1)
    return sum(jnp.where(at == n, value, 0.0) for n, value in columns.items()).astype(i32)


def plan_kernel(where, blocks_ref, plan_ref):
    plan_ref[...] = plan_of(blocks_ref[...], *where())


def pack_kernel(k_ref, v_ref, logit_ref, out_ref):
    logit = logit_ref[...]
    penalty = jnp.maximum(logit, 0.0) + jnp.log(1.0 + jnp.exp(-jnp.abs(logit)))
    upper = penalty.astype(bf16).astype(f32)
    tail = jnp.concatenate([upper, penalty - upper, jnp.zeros((14, SHARD), f32)], axis=0).astype(bf16)
    for j in range(NZ):
        out_ref[j, 0:SHARD, :] = k_ref[0]
        out_ref[j, SHARD : 2 * SHARD, :] = v_ref[0]
        out_ref[j, 2 * SHARD :, :] = tail


def cotangent_kernel(where, g0, g1, g2, g3, w_ref, out_ref, rows):
    xh, core = where()
    pieces = ((xh, core, g0), (1 - xh, core, g1), (xh, 1 - core, g2), (1 - xh, 1 - core, g3))
    for a, b, ref in pieces:
        rows[pl.ds(pl.multiple_of((a * 2 + b) * 32, 32), 32), :] = ref[...]
    for i in range(0, HEADS, 2):
        cot = dot(rows[...], w_ref[i * HD : (i + 2) * HD, :], NT).astype(bf16)
        out_ref[i] = cot[:, :HD]
        out_ref[i + 1] = cot[:, HD:]


def sort_keys(plan_ref, col, kv_ref, ks, vs, pen=None):
    for j in range(NZ):
        low = plan_ref[j, SLOT_AT + col]
        if pen is not None:
            rows = kv_ref[j, 2 * SHARD : 2 * SHARD + 16, :].astype(f32)
            penalty = jnp.broadcast_to(rows[0:1] + rows[1:2], (SHARD, SHARD)).T
        for half, slot in ((0, low), (1, SLOTS - 1 - low)):
            at = pl.ds(pl.multiple_of(slot * HALF, HALF), HALF)
            here = slice(half * HALF, (half + 1) * HALF)
            ks[at, :] = kv_ref[j, here, :]
            vs[at, :] = kv_ref[j, SHARD + half * HALF : SHARD + (half + 1) * HALF, :]
            if pen is not None:
                pen[at, :] = penalty[here, :]


def turn(src, dest):
    for i in range(SLOTS * HALF // SHARD):
        dest[i] = src[i * SHARD : (i + 1) * SHARD, :].astype(f32).T.astype(bf16)


class Part:
    def __init__(self, ref, start):
        self.ref, self.start = ref, start

    def __getitem__(self, i):
        return self.ref[self.start + i]

    def __setitem__(self, i, value):
        self.ref[self.start + i] = value


def list_positions(plan_ref, col, pos):
    for n in range(NZ):
        low = plan_ref[n, POS_AT + col]
        pos[n] = low
        pos[SLOTS - 1 - n] = BLOCKS - 1 - low


def list_steps(plan_ref, col, steps):
    count = jnp.int32(0)
    far = [plan_ref[rh, FAR_AT + col] // STEP for rh in range(QB)]
    for rh in range(QB):
        for c in range(PER_BLOCK):
            steps[count] = rh * PER_BLOCK + c
            count = count + (c < far[rh]).astype(i32)
    plain = count
    for rh in range(QB):
        groups = (plan_ref[rh, SEEN_AT + col] + STEP - 1) // STEP
        for c in range(PER_BLOCK):
            steps[count] = rh * PER_BLOCK + c
            count = count + ((c >= far[rh]) & (c < groups)).astype(i32)
    last = steps[count - 1]
    for i in range(3):
        steps[count + i] = last + SKIP
    return plain, count


def list_streams(plan_ref, col, steps):
    counts = []
    for stream in STREAMS:
        count = jnp.int32(0)
        for rh in range(stream * QS, (stream + 1) * QS):
            groups = (plan_ref[rh, SEEN_AT + col] + STEP - 1) // STEP
            for c in range(PER_BLOCK):
                steps[stream * LIST + count] = rh * PER_BLOCK + c
                count = count + (c < groups).astype(i32)
        last = steps[stream * LIST + count - 1]
        for i in range(5):
            steps[stream * LIST + count + i] = last + SKIP
        counts.append(count)
    count = jnp.maximum(*counts)
    return count + lax.rem(count, 2)


def step_of(steps, t):
    v = steps[t]
    rh = (v // PER_BLOCK) % QB
    c = v % PER_BLOCK
    return v, rh, c, pl.ds(pl.multiple_of(c * CK, CK), CK)


def lists_kernel(plan_ref, *refs):
    for col, ref in enumerate(refs):
        plain, total = list_steps(plan_ref, col, Part(ref, LISTED_AT))

        def note(t, _):
            ref[KEPT_AT + ref[LISTED_AT + t]] = t
            return 0

        lax.fori_loop(0, total, note, 0)
        ref[COUNT_AT] = list_streams(plan_ref, col, ref)
        ref[COUNT_AT + 1] = plain
        ref[COUNT_AT + 2] = total


def stream_step(steps, stream, t):
    v = steps[stream * LIST + t]
    rh = (v // PER_BLOCK) % QB
    c = v % PER_BLOCK
    return v, rh, c, pl.ds(pl.multiple_of(c * CK, CK), CK)


def thresholds(plan_ref, pos, v, rh, c):
    q_block = plan_ref[rh, QBLOCK_AT]
    ahead = [(q_block - pos[c * STEP + i]) * HALF for i in range(STEP)]
    return [(jnp.where(v >= SKIP, HIDDEN, -d), WINDOW - d) for d in ahead]


def offsets():
    shape = (HALF, SHARD)
    return lax.broadcasted_iota(i32, shape, 1) % HALF - lax.broadcasted_iota(i32, shape, 0)


def block_rows(c, i):
    return pl.ds(pl.multiple_of(c * CK + i * HALF, HALF), HALF)


def turned_piece(ref, c):
    n = CK // SHARD
    return jnp.concatenate([ref[c * n + i] for i in range(n)], axis=1)


def load_rows(refs, dest):
    for r, ref in enumerate(refs):
        for half in range(2):
            dest[2 * r + half] = ref[:, half * HALF : (half + 1) * HALF, :].reshape(ROWS, HD)


def forward_kernel(col, plan_ref, *refs):
    if col == 0:
        rows_in, (kv_ref, o_ref, st_ref, peaks, exps, qs, qt), refs = refs[:4], refs[4:11], refs[11:]
    else:
        (qt, kv_ref, lists, o_ref, st_ref, peaks, exps), refs = refs[:7], refs[7:]
    ks, vs, vt, pen, s_a, s_b, f_a, f_b, pos, steps = refs
    list_positions(plan_ref, col, pos)
    if col == 0:
        plain, count = list_steps(plan_ref, col, steps)
    else:
        steps, plain, count = Part(lists, LISTED_AT), lists[COUNT_AT + 1], lists[COUNT_AT + 2]
    if col == 0:
        load_rows(rows_in, qs)
        for rh in range(QB):
            qt[rh] = qs[rh].astype(f32).T.astype(bf16)
    sort_keys(plan_ref, col, kv_ref, ks, vs, pen)
    turn(vs, vt)
    o_ref[...] = jnp.zeros_like(o_ref)
    for rh in range(QB):
        st_ref[rh, 0:1, :] = jnp.full((1, ROWS), LOWEST, f32)
        st_ref[rh, 1:2, :] = jnp.zeros((1, ROWS), f32)
    exps[0] = jnp.zeros_like(exps[0])
    f_b[...] = jnp.ones_like(f_b)

    def score(t, s_ref):
        _, rh, _, at = step_of(steps, t)
        s_ref[...] = dot(ks[at, :], qt[rh], NN)

    def soften(t, s_ref, f_ref, masked):
        v, rh, c, _ = step_of(steps, t)
        limits = thresholds(plan_ref, pos, v, rh, c)
        offset = offsets()
        for lanes in TILES:
            parts = []
            for i, (seen, late) in enumerate(limits):
                s = s_ref[i * HALF : (i + 1) * HALF, lanes] * SCALE
                penalty = pen[block_rows(c, i), :]
                if masked:
                    s = s - jnp.where(offset >= late, penalty, 0.0)
                    parts.append(jnp.where(offset >= seen, s, LOWEST))
                else:
                    parts.append(s - penalty)
            peak = st_ref[rh, 0:1, lanes]
            tops = functools.reduce(jnp.maximum, parts)
            new_peak = jnp.maximum(peak, jnp.max(tops, axis=0, keepdims=True))
            factor = jnp.exp(peak - new_peak)
            parts = [jnp.exp(s - new_peak) for s in parts]
            total = jnp.sum(sum(parts), axis=0, keepdims=True)
            for i, p in enumerate(parts):
                exps[t, i * HALF : (i + 1) * HALF, lanes] = p.astype(bf16)
            f_ref[0:1, lanes] = factor
            peaks[t, 0:1, lanes] = new_peak
            st_ref[rh, 0:1, lanes] = new_peak
            st_ref[rh, 1:2, lanes] = st_ref[rh, 1:2, lanes] * factor + total

    def attend(t, f_ref):
        _, rh, c, _ = step_of(steps, t)
        o_ref[rh] = o_ref[rh] * f_ref[0:1, :] + dot(turned_piece(vt, c), exps[t], NN)

    score(0, s_a)

    def pair(masked, i, _):
        t = 2 * i
        attend(jnp.maximum(t - 1, 0), f_b)
        score(t + 1, s_b)
        soften(t, s_a, f_a, masked)
        attend(t, f_a)
        score(t + 2, s_a)
        soften(t + 1, s_b, f_b, masked)
        return 0

    pairs = (count + 1) // 2
    lax.fori_loop(0, plain // 2, functools.partial(pair, False), 0)
    lax.fori_loop(plain // 2, pairs, functools.partial(pair, True), 0)
    attend(2 * pairs - 1, f_b)


def weigh_kernel(o0, st0, o1, st1, c0, c1, c2, c3, out_ref, cs, ct):
    for r, ref in enumerate((c0, c1, c2, c3)):
        for half in range(2):
            rh = 2 * r + half
            rows = ref[:, half * HALF : (half + 1) * HALF, :].reshape(ROWS, HD)
            cot = rows.astype(f32).T
            cs[rh] = rows
            ct[rh] = cot.astype(bf16)
            peak = jnp.maximum(st0[rh, 0:1, :], st1[rh, 0:1, :])
            f0, f1 = (jnp.exp(st[rh, 0:1, :] - peak) for st in (st0, st1))
            total = st0[rh, 1:2, :] * f0 + st1[rh, 1:2, :] * f1
            seen = total > 0.0
            weighted = jnp.sum(cot * (o0[rh] * f0 + o1[rh] * f1), axis=0, keepdims=True)
            safe = jnp.where(seen, total, 1.0)
            out_ref[rh : rh + 1, :] = jnp.where(seen, peak + jnp.log(safe), LOWEST)
            out_ref[QB + rh : QB + rh + 1, :] = weighted / safe


def combine(parts):
    peak = functools.reduce(jnp.maximum, [norm for norm, _ in parts])
    shares = [jnp.exp(norm - peak) for norm, _ in parts]
    total = sum(shares)
    return peak + jnp.log(total), sum(share * mean for share, (_, mean) in zip(shares, parts)) / total


def row_pair(ref, n):
    return ref[n : n + 1, :], ref[QB + n : QB + n + 1, :]


def merge_stats(pieces, stats):
    for rh in range(QB):
        norm, mean = combine([row_pair(ref, (rh - 2 * t) % QB) for t, ref in enumerate(pieces)])
        stats[rh, 0:1, :] = norm
        stats[rh, 1:2, :] = mean


def backward_kernel(col, plan_ref, steps, *refs):
    (qs, cs, ct, kv_ref, peaks, exps), pieces, refs = refs[:6], refs[6:10], refs[10:]
    if col == 1:
        dq, dkv_ref, refs = refs[:2], refs[2], refs[3:]
    else:
        dq_before, dq_out, dkv_ref, dq, refs = refs[:2], refs[2:6], refs[6], refs[7:9], refs[9:]
        (turned, sems), refs = refs[:2], refs[2:]
    (ks, vs, kt, stats), dk, dv, dl, refs = refs[:4], refs[4:6], refs[6:8], refs[8:10], refs[10:]
    p_even, p_odd, d_even, d_odd, refs = refs[:2], refs[2:4], refs[4:6], refs[6:8], refs[8:]
    (pos,) = refs
    list_positions(plan_ref, col, pos)
    kept_at, count = Part(steps, KEPT_AT), steps[COUNT_AT]
    sort_keys(plan_ref, col, kv_ref, ks, vs)
    turn(ks, kt)
    for ref in dk + dv + dl + p_odd + d_odd:
        ref[...] = jnp.zeros_like(ref)
    for n in STREAMS:
        dq[n][...] = jnp.zeros_like(dq[n]) if col == 1 else dq_before[n][...]
    merge_stats(pieces, stats)

    def differ(n, t, p_refs, d_refs):
        v, rh, c, _ = stream_step(steps, n, t)
        offset = offsets()
        limits = thresholds(plan_ref, pos, v, rh, c)
        kept = kept_at[v % SKIP]
        shares = [jnp.exp(peaks[kept, 0:1, lanes] - stats[rh, 0:1, lanes]) for lanes in TILES]
        shares = [jnp.where(v >= SKIP, 0.0, share) for share in shares]
        for first in range(0, STEP, 2):
            blocks = (first, first + 1)
            late_sums = [dl[n][block_rows(c, i), :] for i in blocks]
            at = pl.ds(pl.multiple_of(c * CK + first * HALF, SHARD), 2 * HALF)
            for wide in WIDE_TILES:
                grad = dot(vs[at, :], ct[rh, :, wide], NN)
                for m, i in enumerate(blocks):
                    rows = slice(i * HALF, (i + 1) * HALF)
                    for j in range(WIDE // SHARD):
                        here = slice(j * SHARD, (j + 1) * SHARD)
                        lanes = slice(wide.start + here.start, wide.start + here.stop)
                        p = exps[kept, rows, lanes].astype(f32) * shares[lanes.start // SHARD]
                        d = p * (grad[m * HALF : (m + 1) * HALF, here] - stats[rh, 1:2, lanes])
                        late_sums[m] = late_sums[m] + jnp.where(offset >= limits[i][1], d, 0.0)
                        p_refs[n][rows, lanes] = p.astype(bf16)
                        d_refs[n][rows, lanes] = d.astype(bf16)
            for m, i in enumerate(blocks):
                dl[n][block_rows(c, i), :] = late_sums[m]

    def gather(n, t, p_refs, d_refs):
        _, rh, c, at = stream_step(steps, n, t)
        dk[n][at, :] += dot(d_refs[n][...], qs[rh], NN)
        dv[n][at, :] += dot(p_refs[n][...], cs[rh], NN)
        dq[n][rh - n * QS] += dot(turned_piece(kt, c), d_refs[n][...], NN)

    def both(work, *args):
        for n in STREAMS:
            work(n, *args)

    def pair(i, _):
        t = 2 * i
        both(gather, jnp.maximum(t - 1, 0), p_odd, d_odd)
        both(differ, t, p_even, d_even)
        both(gather, t, p_even, d_even)
        both(differ, t + 1, p_odd, d_odd)
        return 0

    lax.fori_loop(0, count // 2, pair, 0)
    both(gather, count - 1, p_odd, d_odd)
    copies = []
    if col == 0:
        for r, ref in enumerate(dq_out):
            for half in range(2):
                rows = (dq[r // 2][2 * (r % 2) + half].T * SCALE).astype(bf16)
                turned[r, :, half * HALF : (half + 1) * HALF, :] = rows.reshape(HEADS, HALF, HD)
            copies.append(pltpu.make_async_copy(turned.at[r], ref, sems.at[r]))
            copies[-1].start()
    for j in range(NZ):
        low = plan_ref[j, SLOT_AT + col]
        spots = [pl.ds(pl.multiple_of(slot * HALF, HALF), HALF) for slot in (low, SLOTS - 1 - low)]
        for half, at in enumerate(spots):
            key_sum = (dk[0][at, :] + dk[1][at, :]) * SCALE
            value_sum = dv[0][at, :] + dv[1][at, :]
            dkv_ref[j, half * HALF : (half + 1) * HALF, :] = key_sum.astype(dkv_ref.dtype)
            dkv_ref[j, SHARD + half * HALF : SHARD + (half + 1) * HALF, :] = value_sum.astype(dkv_ref.dtype)
        late = jnp.concatenate([dl[0][at, :] + dl[1][at, :] for at in spots], axis=0)
        total = jnp.sum(late.T, axis=0, keepdims=True)
        dkv_ref[j, 2 * SHARD : 2 * SHARD + 16, :] = jnp.concatenate(
            [total, jnp.zeros((15, SHARD), f32)], axis=0
        ).astype(dkv_ref.dtype)
    for copy in copies:
        copy.wait()


def total_kernel(parts_ref, logit_ref, dk_ref, dv_ref, dl_ref):
    total = parts_ref[0].astype(f32)
    for n in range(1, NZ):
        total = total + parts_ref[n].astype(f32)
    dk_ref[0] = total[:SHARD]
    dv_ref[0] = total[SHARD : 2 * SHARD]
    dl_ref[...] = -jax.nn.sigmoid(logit_ref[...]) * total[2 * SHARD : 2 * SHARD + 1]


VMEM = pl.BlockSpec(memory_space=pltpu.VMEM)
SMEM = pl.BlockSpec(memory_space=pltpu.SMEM)
HBM = pl.BlockSpec(memory_space=pltpu.HBM)


def grant(mib):
    return pltpu.CompilerParams(vmem_limit_bytes=mib * 1024 * 1024)


MOST = 5 * NA
KEYS = SLOTS * HALF
shaped = jax.ShapeDtypeStruct


def cost(us):
    return pl.CostEstimate(flops=int(us * 1e9), bytes_accessed=2**20, transcendentals=0)


def run_plan(where, block_order):
    return pl.pallas_call(
        functools.partial(plan_kernel, where),
        out_shape=shaped((8, SHARD), i32),
        in_specs=[VMEM],
        out_specs=VMEM,
        compiler_params=grant(4),
        cost_estimate=cost(12),
        name="plan",
    )(block_order.T)


def run_pack(keys, values, logits):
    return pl.pallas_call(
        pack_kernel,
        out_shape=shaped((NZ, KV_ROWS, HD), bf16),
        in_specs=[VMEM] * 3,
        out_specs=VMEM,
        compiler_params=grant(4),
        name="pack",
    )(keys, values, logits)


def run_cotangent(where, pieces, w_out):
    return pl.pallas_call(
        functools.partial(cotangent_kernel, where),
        out_shape=shaped((HEADS, SHARD, HD), bf16),
        in_specs=[VMEM] * 5,
        out_specs=VMEM,
        scratch_shapes=[pltpu.VMEM((SHARD, w_out.shape[1]), bf16)],
        compiler_params=grant(8),
        cost_estimate=cost(5),
        name="cotangent",
    )(*pieces, w_out)


def run_forward(col, plan, q, kv, lists=()):
    out_shape = (
        shaped((QB, HD, ROWS), f32),
        shaped((QB, 2, ROWS), f32),
        shaped((MOST, 1, ROWS), f32),
        shaped((MOST, CK, ROWS), bf16),
    )
    if col == 0:
        out_shape += (shaped((QB, ROWS, HD), bf16), shaped((QB, HD, ROWS), bf16))
    o, st, peaks, exps, *turned = pl.pallas_call(
        functools.partial(forward_kernel, col),
        out_shape=out_shape,
        in_specs=[SMEM] + [VMEM] * (len(q) + 1) + [SMEM] * len(lists),
        out_specs=(VMEM,) * len(out_shape),
        scratch_shapes=[
            pltpu.VMEM((KEYS, HD), bf16),
            pltpu.VMEM((KEYS, HD), bf16),
            pltpu.VMEM((KEYS // SHARD, HD, SHARD), bf16),
            pltpu.VMEM((KEYS, SHARD), f32),
            pltpu.VMEM((CK, ROWS), f32),
            pltpu.VMEM((CK, ROWS), f32),
            pltpu.VMEM((8, ROWS), f32),
            pltpu.VMEM((8, ROWS), f32),
            pltpu.SMEM((SLOTS,), i32),
            pltpu.SMEM((QB * PER_BLOCK + 3,), i32),
        ],
        compiler_params=grant(14),
        cost_estimate=cost(10),
        name=f"forward{col}",
    )(plan, *q, kv, *lists)
    return (o, st), (peaks, exps), turned


def run_weigh(sums, cot):
    return pl.pallas_call(
        weigh_kernel,
        out_shape=(
            shaped((2 * QB, ROWS), f32),
            shaped((QB, ROWS, HD), bf16),
            shaped((QB, HD, ROWS), bf16),
        ),
        in_specs=[VMEM] * 8,
        out_specs=(VMEM,) * 3,
        compiler_params=grant(8),
        name="weigh",
    )(*sums, *cot)


def run_backward(col, plan, lists, rows, kv, exps, stats, dq_sum=()):
    sums = [pltpu.VMEM((QS, HD, ROWS), f32)] * 2
    if col == 1:
        scratch = []
        out_shape = (shaped((QS, HD, ROWS), f32),) * 2 + (shaped((NZ, KV_ROWS, HD), bf16),)
        out_specs = (VMEM,) * 3
    else:
        scratch = sums + [
            pltpu.VMEM((NA, HEADS, SHARD, HD), bf16),
            pltpu.SemaphoreType.DMA((NA,)),
        ]
        out_shape = (shaped((HEADS, SHARD, HD), bf16),) * NA + (shaped((NZ, KV_ROWS, HD), f32),)
        out_specs = (HBM,) * NA + (VMEM,)
    return pl.pallas_call(
        functools.partial(backward_kernel, col),
        out_shape=out_shape,
        in_specs=[SMEM] * 2 + [VMEM] * (10 + len(dq_sum)),
        out_specs=out_specs,
        scratch_shapes=scratch
        + [
            pltpu.VMEM((KEYS, HD), bf16),
            pltpu.VMEM((KEYS, HD), bf16),
            pltpu.VMEM((KEYS // SHARD, HD, SHARD), bf16),
            pltpu.VMEM((QB, 2, ROWS), f32),
        ]
        + [pltpu.VMEM((KEYS, HD), f32)] * 6
        + [pltpu.VMEM((CK, ROWS), bf16)] * 8
        + [pltpu.SMEM((SLOTS,), i32)],
        compiler_params=grant(22),
        cost_estimate=cost(15),
        name=f"backward{col}",
    )(plan, lists, *rows, kv, *exps, *stats, *dq_sum)


def run_lists(plan):
    return pl.pallas_call(
        lists_kernel,
        out_shape=(shaped((LISTS,), i32),) * 2,
        in_specs=[SMEM],
        out_specs=(SMEM,) * 2,
        compiler_params=grant(4),
        cost_estimate=cost(2),
        name="lists",
    )(plan)


def run_total(parts, logits):
    return pl.pallas_call(
        total_kernel,
        out_shape=(shaped((1, SHARD, HD), f32), shaped((1, SHARD, HD), f32), shaped((1, SHARD), f32)),
        in_specs=[VMEM] * 2,
        out_specs=(VMEM,) * 3,
        compiler_params=grant(4),
        name="total",
    )(parts, logits)


def from_y(x, r):
    return lax.ppermute(x, "y", [((i + r) % NA, i) for i in range(NA)])


def gather_y(x):
    return [x] + [from_y(x, r) for r in range(1, NA)]


def swap(x, axis):
    return lax.ppermute(x, axis, [(0, 1), (1, 0)])


def place():
    return lax.axis_index("y"), lax.axis_index("z"), lax.axis_index("xl")


def head_place():
    return lax.axis_index("xh"), lax.axis_index("core")


def per_device(queries, keys, values, evict_logits, block_order, grad_y, w_out):
    plan = run_plan(place, block_order)
    keys, plan = lax.optimization_barrier((keys, plan))
    kv = lax.all_to_all(run_pack(keys, values, evict_logits), "z", 0, 0, tiled=True)
    over = swap(grad_y, "xh")
    pieces = (grad_y, over, swap(grad_y, "core"), swap(over, "core"))
    q_all = gather_y(queries)
    cot = run_cotangent(head_place, pieces, w_out)
    kv_other = swap(kv, "xl")
    cot_all = gather_y(cot)
    sums0, exps0, (qs, qt) = run_forward(0, plan, q_all, kv)
    qt, plan = lax.optimization_barrier((qt, plan))
    lists0, lists1 = run_lists(plan)
    sums1, exps1, _ = run_forward(1, plan, (qt,), kv_other, (lists1,))
    stats, cs, ct = run_weigh((*sums0, *sums1), cot_all)
    rows = (qs, cs, ct)
    stats = gather_y(stats)
    *dq_sum, dkv_other = run_backward(1, plan, lists1, rows, kv_other, exps1, stats)
    dkv_here = swap(dkv_other, "xl")
    *dq, dkv = run_backward(0, plan, lists0, rows, kv, exps0, stats, dq_sum)
    dkv = (dkv + dkv_here.astype(f32)).astype(bf16)
    dkv = lax.all_to_all(dkv, "z", 0, 0, tiled=True)
    key_grad, value_grad, logit_grad = run_total(dkv, evict_logits)
    query_grad = dq[0].astype(f32)
    for r in range(1, NA):
        query_grad = query_grad + from_y(dq[r], NA - r).astype(f32)
    return query_grad.astype(bf16), key_grad, value_grad, logit_grad


def solution(mesh):
    split = Mesh(mesh.devices.reshape(4, 8, 2, 2, 2), ("y", "z", "xl", "xh", "core"))
    ctx, head = ("y", "z", "xl"), ("xh", "core")
    return jax.shard_map(
        per_device,
        mesh=split,
        in_specs=(
            P(head, ctx, None),
            P(head, ctx, None),
            P(head, ctx, None),
            P(head, ctx),
            P(),
            P(ctx + head, None),
            P(head, None),
        ),
        out_specs=(
            P(head, ctx, None),
            P(head, ctx, None),
            P(head, ctx, None),
            P(head, ctx),
        ),
        check_vma=False,
    )
```

```python
import functools
import math

import jax
import jax.numpy as jnp
from jax import lax
from jax.experimental import pallas as pl
from jax.experimental.pallas import tpu as pltpu
from jax.sharding import Mesh, PartitionSpec as P

WINDOW = 256
HD = 128
HALF = 64
SHARD = 128
HEADS = 8
ROWS = HEADS * HALF
BLOCKS = 128
LOWEST = -1e30
SCALE = 1.0 / math.sqrt(HD)

NA = 4
NZ = 8
SLOTS = 2 * NZ
QB = 2 * NA
KV_ROWS = 2 * SHARD + 16

STEP = 4
CK = STEP * HALF
PER_BLOCK = SLOTS // STEP
TILES = [slice(j * SHARD, (j + 1) * SHARD) for j in range(ROWS // SHARD)]
WIDE = 256
WIDE_TILES = [slice(j * WIDE, (j + 1) * WIDE) for j in range(ROWS // WIDE)]
STREAMS = (0, 1)
QS = QB // 2
LIST = 24
COUNT_AT, KEPT_AT, LISTED_AT, LISTS = 2 * LIST, 64, 128, 256
SKIP = 64
HIDDEN = 1000

QBLOCK_AT, SEEN_AT, SLOT_AT, POS_AT, FAR_AT = 0, 1, 3, 5, 7
FAR = (WINDOW + 2 * HALF - 2) // HALF

NT = (((1,), (1,)), ((), ()))
NN = (((1,), (0,)), ((), ()))
f32, bf16, i32 = jnp.float32, jnp.bfloat16, jnp.int32


def dot(a, b, dims):
    return lax.dot_general(a, b, dims, preferred_element_type=f32)


def plan_of(blocks, y, z, xl):
    shape = (8, NA * NZ * 2)
    sub = lax.broadcasted_iota(i32, shape, 0)
    lane = lax.broadcasted_iota(i32, shape, 1)
    low = jnp.broadcast_to(blocks[0:1, :].astype(f32), shape)
    high = BLOCKS - 1.0 - low

    def picked(mask, value, axis=1):
        return jnp.sum(jnp.where(mask, value, 0.0), axis=axis, keepdims=True)

    q_low = picked(lane == ((y + (sub >> 1)) & (NA - 1)) * (2 * NZ) + z * 2 + xl, low)
    q_block = jnp.where((sub[:, :1] & 1) == 1, BLOCKS - 1.0 - q_low, q_low)
    columns = {QBLOCK_AT: q_block}
    for col in range(2):
        x = xl if col == 0 else 1 - xl
        here = ((lane >> 4) == y) & ((lane & 1) == x)
        columns[SEEN_AT + col] = picked(here & (low <= q_block), 1.0) + picked(here & (high <= q_block), 1.0)
        far = q_block - FAR
        columns[FAR_AT + col] = picked(here & (low <= far), 1.0) + picked(here & (high <= far), 1.0)
        k_low = picked(here & (((lane >> 1) & (NZ - 1)) == sub), low)
        columns[SLOT_AT + col] = picked(here & (low < k_low), 1.0)
        rank = picked(k_low < low, 1.0, axis=0)
        columns[POS_AT + col] = picked(here & (rank == sub.astype(f32)), low)
    at = lax.broadcasted_iota(i32, (8, SHARD), 1)
    return sum(jnp.where(at == n, value, 0.0) for n, value in columns.items()).astype(i32)


def pack_kernel(where, k_ref, v_ref, logit_ref, blocks_ref, out_ref, plan_ref):
    plan_ref[...] = plan_of(blocks_ref[...], *where())
    logit = logit_ref[...]
    penalty = jnp.maximum(logit, 0.0) + jnp.log(1.0 + jnp.exp(-jnp.abs(logit)))
    upper = penalty.astype(bf16).astype(f32)
    tail = jnp.concatenate([upper, penalty - upper, jnp.zeros((14, SHARD), f32)], axis=0).astype(bf16)
    for j in range(NZ):
        out_ref[j, 0:SHARD, :] = k_ref[0]
        out_ref[j, SHARD : 2 * SHARD, :] = v_ref[0]
        out_ref[j, 2 * SHARD :, :] = tail


def cotangent_kernel(where, g0, g1, g2, g3, w_ref, out_ref, rows):
    xh, core = where()
    pieces = ((xh, core, g0), (1 - xh, core, g1), (xh, 1 - core, g2), (1 - xh, 1 - core, g3))
    for a, b, ref in pieces:
        rows[pl.ds(pl.multiple_of((a * 2 + b) * 32, 32), 32), :] = ref[...]
    for i in range(0, HEADS, 2):
        cot = dot(rows[...], w_ref[i * HD : (i + 2) * HD, :], NT).astype(bf16)
        out_ref[i] = cot[:, :HD]
        out_ref[i + 1] = cot[:, HD:]


def sort_keys(plan_ref, col, kv_ref, ks, vs, pen=None):
    for j in range(NZ):
        low = plan_ref[j, SLOT_AT + col]
        if pen is not None:
            rows = kv_ref[j, 2 * SHARD : 2 * SHARD + 16, :].astype(f32)
            penalty = jnp.broadcast_to(rows[0:1] + rows[1:2], (SHARD, SHARD)).T
        for half, slot in ((0, low), (1, SLOTS - 1 - low)):
            at = pl.ds(pl.multiple_of(slot * HALF, HALF), HALF)
            here = slice(half * HALF, (half + 1) * HALF)
            ks[at, :] = kv_ref[j, here, :]
            vs[at, :] = kv_ref[j, SHARD + half * HALF : SHARD + (half + 1) * HALF, :]
            if pen is not None:
                pen[at, :] = penalty[here, :]


def turn(src, dest):
    for i in range(SLOTS * HALF // SHARD):
        dest[i] = src[i * SHARD : (i + 1) * SHARD, :].astype(f32).T.astype(bf16)


class Part:
    def __init__(self, ref, start):
        self.ref, self.start = ref, start

    def __getitem__(self, i):
        return self.ref[self.start + i]

    def __setitem__(self, i, value):
        self.ref[self.start + i] = value


def list_positions(plan_ref, col, pos):
    for n in range(NZ):
        low = plan_ref[n, POS_AT + col]
        pos[n] = low
        pos[SLOTS - 1 - n] = BLOCKS - 1 - low


def list_steps(plan_ref, col, steps):
    count = jnp.int32(0)
    far = [plan_ref[rh, FAR_AT + col] // STEP for rh in range(QB)]
    for rh in range(QB):
        for c in range(PER_BLOCK):
            steps[count] = rh * PER_BLOCK + c
            count = count + (c < far[rh]).astype(i32)
    plain = count
    for rh in range(QB):
        groups = (plan_ref[rh, SEEN_AT + col] + STEP - 1) // STEP
        for c in range(PER_BLOCK):
            steps[count] = rh * PER_BLOCK + c
            count = count + ((c >= far[rh]) & (c < groups)).astype(i32)
    last = steps[count - 1]
    for i in range(3):
        steps[count + i] = last + SKIP
    return plain, count


def list_streams(plan_ref, col, steps):
    counts = []
    for stream in STREAMS:
        count = jnp.int32(0)
        for rh in range(stream * QS, (stream + 1) * QS):
            groups = (plan_ref[rh, SEEN_AT + col] + STEP - 1) // STEP
            for c in range(PER_BLOCK):
                steps[stream * LIST + count] = rh * PER_BLOCK + c
                count = count + (c < groups).astype(i32)
        last = steps[stream * LIST + count - 1]
        for i in range(5):
            steps[stream * LIST + count + i] = last + SKIP
        counts.append(count)
    count = jnp.maximum(*counts)
    return count + lax.rem(count, 2)


def step_of(steps, t):
    v = steps[t]
    rh = (v // PER_BLOCK) % QB
    c = v % PER_BLOCK
    return v, rh, c, pl.ds(pl.multiple_of(c * CK, CK), CK)


def lists_kernel(plan_ref, *refs):
    for col, ref in enumerate(refs):
        plain, total = list_steps(plan_ref, col, Part(ref, LISTED_AT))

        def note(t, _):
            ref[KEPT_AT + ref[LISTED_AT + t]] = t
            return 0

        lax.fori_loop(0, total, note, 0)
        ref[COUNT_AT] = list_streams(plan_ref, col, ref)
        ref[COUNT_AT + 1] = plain
        ref[COUNT_AT + 2] = total


def stream_step(steps, stream, t):
    v = steps[stream * LIST + t]
    rh = (v // PER_BLOCK) % QB
    c = v % PER_BLOCK
    return v, rh, c, pl.ds(pl.multiple_of(c * CK, CK), CK)


def thresholds(plan_ref, pos, v, rh, c):
    q_block = plan_ref[rh, QBLOCK_AT]
    ahead = [(q_block - pos[c * STEP + i]) * HALF for i in range(STEP)]
    return [(jnp.where(v >= SKIP, HIDDEN, -d), WINDOW - d) for d in ahead]


def offsets():
    shape = (HALF, SHARD)
    return lax.broadcasted_iota(i32, shape, 1) % HALF - lax.broadcasted_iota(i32, shape, 0)


def block_rows(c, i):
    return pl.ds(pl.multiple_of(c * CK + i * HALF, HALF), HALF)


def turned_piece(ref, c):
    n = CK // SHARD
    return jnp.concatenate([ref[c * n + i] for i in range(n)], axis=1)


def load_rows(refs, dest):
    for r, ref in enumerate(refs):
        for half in range(2):
            dest[2 * r + half] = ref[:, half * HALF : (half + 1) * HALF, :].reshape(ROWS, HD)


def forward_kernel(col, plan_ref, *refs):
    if col == 0:
        rows_in, (kv_ref, o_ref, st_ref, peaks, exps, qs, qt), refs = refs[:4], refs[4:11], refs[11:]
    else:
        (qt, kv_ref, lists, o_ref, st_ref, peaks, exps), refs = refs[:7], refs[7:]
    ks, vs, vt, pen, s_a, s_b, f_a, f_b, pos, steps = refs
    list_positions(plan_ref, col, pos)
    if col == 0:
        plain, count = list_steps(plan_ref, col, steps)
    else:
        steps, plain, count = Part(lists, LISTED_AT), lists[COUNT_AT + 1], lists[COUNT_AT + 2]
    if col == 0:
        load_rows(rows_in, qs)
        for rh in range(QB):
            qt[rh] = qs[rh].astype(f32).T.astype(bf16)
    sort_keys(plan_ref, col, kv_ref, ks, vs, pen)
    turn(vs, vt)
    o_ref[...] = jnp.zeros_like(o_ref)
    for rh in range(QB):
        st_ref[rh, 0:1, :] = jnp.full((1, ROWS), LOWEST, f32)
        st_ref[rh, 1:2, :] = jnp.zeros((1, ROWS), f32)
    exps[0] = jnp.zeros_like(exps[0])
    f_b[...] = jnp.ones_like(f_b)

    def score(t, s_ref):
        _, rh, _, at = step_of(steps, t)
        s_ref[...] = dot(ks[at, :], qt[rh], NN)

    def soften(t, s_ref, f_ref, masked):
        v, rh, c, _ = step_of(steps, t)
        limits = thresholds(plan_ref, pos, v, rh, c)
        offset = offsets()
        for lanes in TILES:
            parts = []
            for i, (seen, late) in enumerate(limits):
                s = s_ref[i * HALF : (i + 1) * HALF, lanes] * SCALE
                penalty = pen[block_rows(c, i), :]
                if masked:
                    s = s - jnp.where(offset >= late, penalty, 0.0)
                    parts.append(jnp.where(offset >= seen, s, LOWEST))
                else:
                    parts.append(s - penalty)
            peak = st_ref[rh, 0:1, lanes]
            tops = functools.reduce(jnp.maximum, parts)
            new_peak = jnp.maximum(peak, jnp.max(tops, axis=0, keepdims=True))
            factor = jnp.exp(peak - new_peak)
            parts = [jnp.exp(s - new_peak) for s in parts]
            total = jnp.sum(sum(parts), axis=0, keepdims=True)
            for i, p in enumerate(parts):
                exps[t, i * HALF : (i + 1) * HALF, lanes] = p.astype(bf16)
            f_ref[0:1, lanes] = factor
            peaks[t, 0:1, lanes] = new_peak
            st_ref[rh, 0:1, lanes] = new_peak
            st_ref[rh, 1:2, lanes] = st_ref[rh, 1:2, lanes] * factor + total

    def attend(t, f_ref):
        _, rh, c, _ = step_of(steps, t)
        o_ref[rh] = o_ref[rh] * f_ref[0:1, :] + dot(turned_piece(vt, c), exps[t], NN)

    score(0, s_a)

    def pair(masked, i, _):
        t = 2 * i
        attend(jnp.maximum(t - 1, 0), f_b)
        score(t + 1, s_b)
        soften(t, s_a, f_a, masked)
        attend(t, f_a)
        score(t + 2, s_a)
        soften(t + 1, s_b, f_b, masked)
        return 0

    pairs = (count + 1) // 2
    lax.fori_loop(0, plain // 2, functools.partial(pair, False), 0)
    lax.fori_loop(plain // 2, pairs, functools.partial(pair, True), 0)
    attend(2 * pairs - 1, f_b)


def weigh_kernel(o0, st0, o1, st1, c0, c1, c2, c3, out_ref, cs, ct):
    for r, ref in enumerate((c0, c1, c2, c3)):
        for half in range(2):
            rh = 2 * r + half
            rows = ref[:, half * HALF : (half + 1) * HALF, :].reshape(ROWS, HD)
            cot = rows.astype(f32).T
            cs[rh] = rows
            ct[rh] = cot.astype(bf16)
            peak = jnp.maximum(st0[rh, 0:1, :], st1[rh, 0:1, :])
            f0, f1 = (jnp.exp(st[rh, 0:1, :] - peak) for st in (st0, st1))
            total = st0[rh, 1:2, :] * f0 + st1[rh, 1:2, :] * f1
            seen = total > 0.0
            weighted = jnp.sum(cot * (o0[rh] * f0 + o1[rh] * f1), axis=0, keepdims=True)
            safe = jnp.where(seen, total, 1.0)
            out_ref[rh : rh + 1, :] = jnp.where(seen, peak + jnp.log(safe), LOWEST)
            out_ref[QB + rh : QB + rh + 1, :] = weighted / safe


def combine(parts):
    peak = functools.reduce(jnp.maximum, [norm for norm, _ in parts])
    shares = [jnp.exp(norm - peak) for norm, _ in parts]
    total = sum(shares)
    return peak + jnp.log(total), sum(share * mean for share, (_, mean) in zip(shares, parts)) / total


def row_pair(ref, n):
    return ref[n : n + 1, :], ref[QB + n : QB + n + 1, :]


def merge_stats(pieces, stats):
    for rh in range(QB):
        norm, mean = combine([row_pair(ref, (rh - 2 * t) % QB) for t, ref in enumerate(pieces)])
        stats[rh, 0:1, :] = norm
        stats[rh, 1:2, :] = mean


def ready_kernel(plan_ref, kv0, kv1, vs0, kt0, vs1, kt1, ks):
    for col, kv_ref, vs, kt in ((0, kv0, vs0, kt0), (1, kv1, vs1, kt1)):
        sort_keys(plan_ref, col, kv_ref, ks, vs)
        turn(ks, kt)


def backward_kernel(col, plan_ref, steps, *refs):
    (qs, cs, ct, vs, kt, peaks, exps), pieces, refs = refs[:7], refs[7:11], refs[11:]
    if col == 1:
        dq, dkv_ref, refs = refs[:2], refs[2], refs[3:]
    else:
        dq_before, dq_out, dkv_ref, dq, refs = refs[:2], refs[2:6], refs[6], refs[7:9], refs[9:]
        (turned, sems), refs = refs[:2], refs[2:]
    stats, dk, dv, dl, refs = refs[0], refs[1:3], refs[3:5], refs[5:7], refs[7:]
    p_even, p_odd, d_even, d_odd, refs = refs[:2], refs[2:4], refs[4:6], refs[6:8], refs[8:]
    (pos,) = refs
    list_positions(plan_ref, col, pos)
    kept_at, count = Part(steps, KEPT_AT), steps[COUNT_AT]
    for ref in dk + dv + dl + p_odd + d_odd:
        ref[...] = jnp.zeros_like(ref)
    for n in STREAMS:
        dq[n][...] = jnp.zeros_like(dq[n]) if col == 1 else dq_before[n][...]
    merge_stats(pieces, stats)

    def differ(n, t, p_refs, d_refs):
        v, rh, c, _ = stream_step(steps, n, t)
        offset = offsets()
        limits = thresholds(plan_ref, pos, v, rh, c)
        kept = kept_at[v % SKIP]
        shares = [jnp.exp(peaks[kept, 0:1, lanes] - stats[rh, 0:1, lanes]) for lanes in TILES]
        shares = [jnp.where(v >= SKIP, 0.0, share) for share in shares]
        for first in range(0, STEP, 2):
            blocks = (first, first + 1)
            late_sums = [dl[n][block_rows(c, i), :] for i in blocks]
            at = pl.ds(pl.multiple_of(c * CK + first * HALF, SHARD), 2 * HALF)
            for wide in WIDE_TILES:
                grad = dot(vs[at, :], ct[rh, :, wide], NN)
                for m, i in enumerate(blocks):
                    rows = slice(i * HALF, (i + 1) * HALF)
                    for j in range(WIDE // SHARD):
                        here = slice(j * SHARD, (j + 1) * SHARD)
                        lanes = slice(wide.start + here.start, wide.start + here.stop)
                        p = exps[kept, rows, lanes].astype(f32) * shares[lanes.start // SHARD]
                        d = p * (grad[m * HALF : (m + 1) * HALF, here] - stats[rh, 1:2, lanes])
                        late_sums[m] = late_sums[m] + jnp.where(offset >= limits[i][1], d, 0.0)
                        p_refs[n][rows, lanes] = p.astype(bf16)
                        d_refs[n][rows, lanes] = d.astype(bf16)
            for m, i in enumerate(blocks):
                dl[n][block_rows(c, i), :] = late_sums[m]

    def gather(n, t, p_refs, d_refs):
        _, rh, c, at = stream_step(steps, n, t)
        dk[n][at, :] += dot(d_refs[n][...], qs[rh], NN)
        dv[n][at, :] += dot(p_refs[n][...], cs[rh], NN)
        dq[n][rh - n * QS] += dot(turned_piece(kt, c), d_refs[n][...], NN)

    def both(work, *args):
        for n in STREAMS:
            work(n, *args)

    def pair(i, _):
        t = 2 * i
        both(gather, jnp.maximum(t - 1, 0), p_odd, d_odd)
        both(differ, t, p_even, d_even)
        both(gather, t, p_even, d_even)
        both(differ, t + 1, p_odd, d_odd)
        return 0

    lax.fori_loop(0, count // 2, pair, 0)
    both(gather, count - 1, p_odd, d_odd)
    copies = []
    if col == 0:
        for r, ref in enumerate(dq_out):
            for half in range(2):
                rows = (dq[r // 2][2 * (r % 2) + half].T * SCALE).astype(bf16)
                turned[r, :, half * HALF : (half + 1) * HALF, :] = rows.reshape(HEADS, HALF, HD)
            copies.append(pltpu.make_async_copy(turned.at[r], ref, sems.at[r]))
            copies[-1].start()
    for j in range(NZ):
        low = plan_ref[j, SLOT_AT + col]
        spots = [pl.ds(pl.multiple_of(slot * HALF, HALF), HALF) for slot in (low, SLOTS - 1 - low)]
        for half, at in enumerate(spots):
            key_sum = (dk[0][at, :] + dk[1][at, :]) * SCALE
            value_sum = dv[0][at, :] + dv[1][at, :]
            dkv_ref[j, half * HALF : (half + 1) * HALF, :] = key_sum.astype(dkv_ref.dtype)
            dkv_ref[j, SHARD + half * HALF : SHARD + (half + 1) * HALF, :] = value_sum.astype(dkv_ref.dtype)
        late = jnp.concatenate([dl[0][at, :] + dl[1][at, :] for at in spots], axis=0)
        total = jnp.sum(late.T, axis=0, keepdims=True)
        dkv_ref[j, 2 * SHARD : 2 * SHARD + 16, :] = jnp.concatenate(
            [total, jnp.zeros((15, SHARD), f32)], axis=0
        ).astype(dkv_ref.dtype)
    for copy in copies:
        copy.wait()


def total_kernel(parts_ref, logit_ref, dk_ref, dv_ref, dl_ref):
    total = parts_ref[0].astype(f32)
    for n in range(1, NZ):
        total = total + parts_ref[n].astype(f32)
    dk_ref[0] = total[:SHARD]
    dv_ref[0] = total[SHARD : 2 * SHARD]
    dl_ref[...] = -jax.nn.sigmoid(logit_ref[...]) * total[2 * SHARD : 2 * SHARD + 1]


VMEM = pl.BlockSpec(memory_space=pltpu.VMEM)
SMEM = pl.BlockSpec(memory_space=pltpu.SMEM)
HBM = pl.BlockSpec(memory_space=pltpu.HBM)


def grant(mib):
    return pltpu.CompilerParams(vmem_limit_bytes=mib * 1024 * 1024)


MOST = 5 * NA
KEYS = SLOTS * HALF
shaped = jax.ShapeDtypeStruct


def cost(us):
    return pl.CostEstimate(flops=int(us * 1e9), bytes_accessed=2**20, transcendentals=0)


def run_pack(where, keys, values, logits, block_order):
    return pl.pallas_call(
        functools.partial(pack_kernel, where),
        out_shape=(shaped((NZ, KV_ROWS, HD), bf16), shaped((8, SHARD), i32)),
        in_specs=[VMEM] * 4,
        out_specs=(VMEM, VMEM),
        name="pack",
    )(keys, values, logits, block_order.T)


def run_cotangent(where, pieces, w_out):
    return pl.pallas_call(
        functools.partial(cotangent_kernel, where),
        out_shape=shaped((HEADS, SHARD, HD), bf16),
        in_specs=[VMEM] * 5,
        out_specs=VMEM,
        scratch_shapes=[pltpu.VMEM((SHARD, w_out.shape[1]), bf16)],
        compiler_params=grant(8),
        cost_estimate=cost(5),
        name="cotangent",
    )(*pieces, w_out)


def run_forward(col, plan, q, kv, lists=()):
    out_shape = (
        shaped((QB, HD, ROWS), f32),
        shaped((QB, 2, ROWS), f32),
        shaped((MOST, 1, ROWS), f32),
        shaped((MOST, CK, ROWS), bf16),
    )
    if col == 0:
        out_shape += (shaped((QB, ROWS, HD), bf16), shaped((QB, HD, ROWS), bf16))
    o, st, peaks, exps, *turned = pl.pallas_call(
        functools.partial(forward_kernel, col),
        out_shape=out_shape,
        in_specs=[SMEM] + [VMEM] * (len(q) + 1) + [SMEM] * len(lists),
        out_specs=(VMEM,) * len(out_shape),
        scratch_shapes=[
            pltpu.VMEM((KEYS, HD), bf16),
            pltpu.VMEM((KEYS, HD), bf16),
            pltpu.VMEM((KEYS // SHARD, HD, SHARD), bf16),
            pltpu.VMEM((KEYS, SHARD), f32),
            pltpu.VMEM((CK, ROWS), f32),
            pltpu.VMEM((CK, ROWS), f32),
            pltpu.VMEM((8, ROWS), f32),
            pltpu.VMEM((8, ROWS), f32),
            pltpu.SMEM((SLOTS,), i32),
            pltpu.SMEM((QB * PER_BLOCK + 3,), i32),
        ],
        compiler_params=grant(14),
        cost_estimate=cost(10),
        name=f"forward{col}",
    )(plan, *q, kv, *lists)
    return (o, st), (peaks, exps), turned


def run_weigh(sums, cot):
    return pl.pallas_call(
        weigh_kernel,
        out_shape=(
            shaped((2 * QB, ROWS), f32),
            shaped((QB, ROWS, HD), bf16),
            shaped((QB, HD, ROWS), bf16),
        ),
        in_specs=[VMEM] * 8,
        out_specs=(VMEM,) * 3,
        compiler_params=grant(8),
        name="weigh",
    )(*sums, *cot)


def run_backward(col, plan, lists, rows, ready, exps, stats, dq_sum=()):
    sums = [pltpu.VMEM((QS, HD, ROWS), f32)] * 2
    if col == 1:
        scratch = []
        out_shape = (shaped((QS, HD, ROWS), f32),) * 2 + (shaped((NZ, KV_ROWS, HD), bf16),)
        out_specs = (VMEM,) * 3
    else:
        scratch = sums + [
            pltpu.VMEM((NA, HEADS, SHARD, HD), bf16),
            pltpu.SemaphoreType.DMA((NA,)),
        ]
        out_shape = (shaped((HEADS, SHARD, HD), bf16),) * NA + (shaped((NZ, KV_ROWS, HD), f32),)
        out_specs = (HBM,) * NA + (VMEM,)
    return pl.pallas_call(
        functools.partial(backward_kernel, col),
        out_shape=out_shape,
        in_specs=[SMEM] * 2 + [VMEM] * (11 + len(dq_sum)),
        out_specs=out_specs,
        scratch_shapes=scratch
        + [pltpu.VMEM((QB, 2, ROWS), f32)]
        + [pltpu.VMEM((KEYS, HD), f32)] * 6
        + [pltpu.VMEM((CK, ROWS), bf16)] * 8
        + [pltpu.SMEM((SLOTS,), i32)],
        compiler_params=grant(22),
        cost_estimate=cost(15),
        name=f"backward{col}",
    )(plan, lists, *rows, *ready, *exps, *stats, *dq_sum)


def run_lists(plan):
    return pl.pallas_call(
        lists_kernel,
        out_shape=(shaped((LISTS,), i32),) * 2,
        in_specs=[SMEM],
        out_specs=(SMEM,) * 2,
        compiler_params=grant(4),
        cost_estimate=cost(2),
        name="lists",
    )(plan)


def run_ready(plan, kv0, kv1):
    shapes = (shaped((KEYS, HD), bf16), shaped((KEYS // SHARD, HD, SHARD), bf16))
    out = pl.pallas_call(
        ready_kernel,
        out_shape=shapes * 2,
        in_specs=[SMEM] + [VMEM] * 2,
        out_specs=(VMEM,) * 4,
        scratch_shapes=[pltpu.VMEM((KEYS, HD), bf16)],
        compiler_params=grant(4),
        cost_estimate=cost(2),
        name="ready",
    )(plan, kv0, kv1)
    return out[:2], out[2:]


def run_total(parts, logits):
    return pl.pallas_call(
        total_kernel,
        out_shape=(shaped((1, SHARD, HD), f32), shaped((1, SHARD, HD), f32), shaped((1, SHARD), f32)),
        in_specs=[VMEM] * 2,
        out_specs=(VMEM,) * 3,
        compiler_params=grant(4),
        name="total",
    )(parts, logits)


def from_y(x, r):
    return lax.ppermute(x, "y", [((i + r) % NA, i) for i in range(NA)])


def gather_y(x):
    return [x] + [from_y(x, r) for r in range(1, NA)]


def swap(x, axis):
    return lax.ppermute(x, axis, [(0, 1), (1, 0)])


def place():
    return lax.axis_index("y"), lax.axis_index("z"), lax.axis_index("xl")


def head_place():
    return lax.axis_index("xh"), lax.axis_index("core")


def per_device(queries, keys, values, evict_logits, block_order, grad_y, w_out):
    packed, plan = run_pack(place, keys, values, evict_logits, block_order)
    kv = lax.all_to_all(packed, "z", 0, 0, tiled=True)
    over = swap(grad_y, "xh")
    pieces = (grad_y, over, swap(grad_y, "core"), swap(over, "core"))
    q_all = gather_y(queries)
    cot = run_cotangent(head_place, pieces, w_out)
    kv_other = swap(kv, "xl")
    cot_all = gather_y(cot)
    sums0, exps0, (qs, qt) = run_forward(0, plan, q_all, kv)
    qt, plan = lax.optimization_barrier((qt, plan))
    lists0, lists1 = run_lists(plan)
    sums1, exps1, _ = run_forward(1, plan, (qt,), kv_other, (lists1,))
    stats, cs, ct = run_weigh((*sums0, *sums1), cot_all)
    rows = (qs, cs, ct)
    stats, kv_other = lax.optimization_barrier((stats, kv_other))
    ready0, ready1 = run_ready(plan, kv, kv_other)
    stats = gather_y(stats)
    *dq_sum, dkv_other = run_backward(1, plan, lists1, rows, ready1, exps1, stats)
    dkv_here = swap(dkv_other, "xl")
    *dq, dkv = run_backward(0, plan, lists0, rows, ready0, exps0, stats, dq_sum)
    dkv = (dkv + dkv_here.astype(f32)).astype(bf16)
    dkv = lax.all_to_all(dkv, "z", 0, 0, tiled=True)
    key_grad, value_grad, logit_grad = run_total(dkv, evict_logits)
    query_grad = dq[0].astype(f32)
    for r in range(1, NA):
        query_grad = query_grad + from_y(dq[r], NA - r).astype(f32)
    return query_grad.astype(bf16), key_grad, value_grad, logit_grad


def solution(mesh):
    split = Mesh(mesh.devices.reshape(4, 8, 2, 2, 2), ("y", "z", "xl", "xh", "core"))
    ctx, head = ("y", "z", "xl"), ("xh", "core")
    return jax.shard_map(
        per_device,
        mesh=split,
        in_specs=(
            P(head, ctx, None),
            P(head, ctx, None),
            P(head, ctx, None),
            P(head, ctx),
            P(),
            P(ctx + head, None),
            P(head, None),
        ),
        out_specs=(
            P(head, ctx, None),
            P(head, ctx, None),
            P(head, ctx, None),
            P(head, ctx),
        ),
        check_vma=False,
    )
```

```python
import functools
import math

import jax
import jax.numpy as jnp
from jax import lax
from jax.experimental import pallas as pl
from jax.experimental.pallas import tpu as pltpu
from jax.sharding import Mesh, PartitionSpec as P

WINDOW = 256
HD = 128
HALF = 64
SHARD = 128
HEADS = 8
ROWS = HEADS * HALF
BLOCKS = 128
LOWEST = -1e30
SCALE = 1.0 / math.sqrt(HD)

NA = 4
NZ = 8
SLOTS = 2 * NZ
QB = 2 * NA
KV_ROWS = 2 * SHARD + 16

STEP = 4
CK = STEP * HALF
PER_BLOCK = SLOTS // STEP
TILES = [slice(j * SHARD, (j + 1) * SHARD) for j in range(ROWS // SHARD)]
WIDE = 256
WIDE_TILES = [slice(j * WIDE, (j + 1) * WIDE) for j in range(ROWS // WIDE)]
STREAMS = (0, 1)
QS = QB // 2
LIST = 24
COUNT_AT, KEPT_AT, LISTED_AT, LISTS = 2 * LIST, 64, 128, 256
SKIP = 64
HIDDEN = 1000

QBLOCK_AT, SEEN_AT, SLOT_AT, POS_AT, FAR_AT = 0, 1, 3, 5, 7
FAR = (WINDOW + 2 * HALF - 2) // HALF

NT = (((1,), (1,)), ((), ()))
NN = (((1,), (0,)), ((), ()))
f32, bf16, i32 = jnp.float32, jnp.bfloat16, jnp.int32


def dot(a, b, dims):
    return lax.dot_general(a, b, dims, preferred_element_type=f32)


def plan_of(blocks, y, z, xl):
    shape = (8, NA * NZ * 2)
    sub = lax.broadcasted_iota(i32, shape, 0)
    lane = lax.broadcasted_iota(i32, shape, 1)
    low = jnp.broadcast_to(blocks[0:1, :].astype(f32), shape)
    high = BLOCKS - 1.0 - low

    def picked(mask, value, axis=1):
        return jnp.sum(jnp.where(mask, value, 0.0), axis=axis, keepdims=True)

    q_low = picked(lane == ((y + (sub >> 1)) & (NA - 1)) * (2 * NZ) + z * 2 + xl, low)
    q_block = jnp.where((sub[:, :1] & 1) == 1, BLOCKS - 1.0 - q_low, q_low)
    columns = {QBLOCK_AT: q_block}
    for col in range(2):
        x = xl if col == 0 else 1 - xl
        here = ((lane >> 4) == y) & ((lane & 1) == x)
        columns[SEEN_AT + col] = picked(here & (low <= q_block), 1.0) + picked(here & (high <= q_block), 1.0)
        far = q_block - FAR
        columns[FAR_AT + col] = picked(here & (low <= far), 1.0) + picked(here & (high <= far), 1.0)
        k_low = picked(here & (((lane >> 1) & (NZ - 1)) == sub), low)
        columns[SLOT_AT + col] = picked(here & (low < k_low), 1.0)
        rank = picked(k_low < low, 1.0, axis=0)
        columns[POS_AT + col] = picked(here & (rank == sub.astype(f32)), low)
    at = lax.broadcasted_iota(i32, (8, SHARD), 1)
    return sum(jnp.where(at == n, value, 0.0) for n, value in columns.items()).astype(i32)


def plan_kernel(where, blocks_ref, plan_ref):
    plan_ref[...] = plan_of(blocks_ref[...], *where())


def pack_kernel(k_ref, v_ref, logit_ref, out_ref):
    logit = logit_ref[...]
    penalty = jnp.maximum(logit, 0.0) + jnp.log(1.0 + jnp.exp(-jnp.abs(logit)))
    upper = penalty.astype(bf16).astype(f32)
    tail = jnp.concatenate([upper, penalty - upper, jnp.zeros((14, SHARD), f32)], axis=0).astype(bf16)
    for j in range(NZ):
        out_ref[j, 0:SHARD, :] = k_ref[0]
        out_ref[j, SHARD : 2 * SHARD, :] = v_ref[0]
        out_ref[j, 2 * SHARD :, :] = tail


def cotangent_kernel(where, g0, g1, g2, g3, w_ref, out_ref, rows):
    xh, core = where()
    pieces = ((xh, core, g0), (1 - xh, core, g1), (xh, 1 - core, g2), (1 - xh, 1 - core, g3))
    for a, b, ref in pieces:
        rows[pl.ds(pl.multiple_of((a * 2 + b) * 32, 32), 32), :] = ref[...]
    for i in range(0, HEADS, 2):
        cot = dot(rows[...], w_ref[i * HD : (i + 2) * HD, :], NT).astype(bf16)
        out_ref[i] = cot[:, :HD]
        out_ref[i + 1] = cot[:, HD:]


def sort_keys(plan_ref, col, kv_ref, ks, vs, pen=None):
    for j in range(NZ):
        low = plan_ref[j, SLOT_AT + col]
        if pen is not None:
            rows = kv_ref[j, 2 * SHARD : 2 * SHARD + 16, :].astype(f32)
            penalty = jnp.broadcast_to(rows[0:1] + rows[1:2], (SHARD, SHARD)).T
        for half, slot in ((0, low), (1, SLOTS - 1 - low)):
            at = pl.ds(pl.multiple_of(slot * HALF, HALF), HALF)
            here = slice(half * HALF, (half + 1) * HALF)
            ks[at, :] = kv_ref[j, here, :]
            vs[at, :] = kv_ref[j, SHARD + half * HALF : SHARD + (half + 1) * HALF, :]
            if pen is not None:
                pen[at, :] = penalty[here, :]


def turn(src, dest):
    for i in range(SLOTS * HALF // SHARD):
        dest[i] = src[i * SHARD : (i + 1) * SHARD, :].astype(f32).T.astype(bf16)


class Part:
    def __init__(self, ref, start):
        self.ref, self.start = ref, start

    def __getitem__(self, i):
        return self.ref[self.start + i]

    def __setitem__(self, i, value):
        self.ref[self.start + i] = value


def list_positions(plan_ref, col, pos):
    for n in range(NZ):
        low = plan_ref[n, POS_AT + col]
        pos[n] = low
        pos[SLOTS - 1 - n] = BLOCKS - 1 - low


def list_steps(plan_ref, col, steps):
    count = jnp.int32(0)
    far = [plan_ref[rh, FAR_AT + col] // STEP for rh in range(QB)]
    for rh in range(QB):
        for c in range(PER_BLOCK):
            steps[count] = rh * PER_BLOCK + c
            count = count + (c < far[rh]).astype(i32)
    plain = count
    for rh in range(QB):
        groups = (plan_ref[rh, SEEN_AT + col] + STEP - 1) // STEP
        for c in range(PER_BLOCK):
            steps[count] = rh * PER_BLOCK + c
            count = count + ((c >= far[rh]) & (c < groups)).astype(i32)
    last = steps[count - 1]
    for i in range(3):
        steps[count + i] = last + SKIP
    return plain, count


def list_streams(plan_ref, col, steps):
    counts = []
    for stream in STREAMS:
        count = jnp.int32(0)
        for rh in range(stream * QS, (stream + 1) * QS):
            groups = (plan_ref[rh, SEEN_AT + col] + STEP - 1) // STEP
            for c in range(PER_BLOCK):
                steps[stream * LIST + count] = rh * PER_BLOCK + c
                count = count + (c < groups).astype(i32)
        last = steps[stream * LIST + count - 1]
        for i in range(5):
            steps[stream * LIST + count + i] = last + SKIP
        counts.append(count)
    count = jnp.maximum(*counts)
    return count + lax.rem(count, 2)


def step_of(steps, t):
    v = steps[t]
    rh = (v // PER_BLOCK) % QB
    c = v % PER_BLOCK
    return v, rh, c, pl.ds(pl.multiple_of(c * CK, CK), CK)


def lists_kernel(plan_ref, *refs):
    for col, ref in enumerate(refs):
        plain, total = list_steps(plan_ref, col, Part(ref, LISTED_AT))

        def note(t, _):
            ref[KEPT_AT + ref[LISTED_AT + t]] = t
            return 0

        lax.fori_loop(0, total, note, 0)
        ref[COUNT_AT] = list_streams(plan_ref, col, ref)
        ref[COUNT_AT + 1] = plain
        ref[COUNT_AT + 2] = total


def stream_step(steps, stream, t):
    v = steps[stream * LIST + t]
    rh = (v // PER_BLOCK) % QB
    c = v % PER_BLOCK
    return v, rh, c, pl.ds(pl.multiple_of(c * CK, CK), CK)


def thresholds(plan_ref, pos, v, rh, c):
    q_block = plan_ref[rh, QBLOCK_AT]
    ahead = [(q_block - pos[c * STEP + i]) * HALF for i in range(STEP)]
    return [(jnp.where(v >= SKIP, HIDDEN, -d), WINDOW - d) for d in ahead]


def offsets():
    shape = (HALF, SHARD)
    return lax.broadcasted_iota(i32, shape, 1) % HALF - lax.broadcasted_iota(i32, shape, 0)


def block_rows(c, i):
    return pl.ds(pl.multiple_of(c * CK + i * HALF, HALF), HALF)


def turned_piece(ref, c):
    n = CK // SHARD
    return jnp.concatenate([ref[c * n + i] for i in range(n)], axis=1)


def load_rows(refs, dest):
    for r, ref in enumerate(refs):
        for half in range(2):
            dest[2 * r + half] = ref[:, half * HALF : (half + 1) * HALF, :].reshape(ROWS, HD)


def forward_kernel(col, plan_ref, *refs):
    if col == 0:
        rows_in, (kv_ref, o_ref, st_ref, peaks, exps, qs, qt), refs = refs[:4], refs[4:11], refs[11:]
    else:
        (qt, kv_ref, lists, o_ref, st_ref, peaks, exps), refs = refs[:7], refs[7:]
    ks, vs, vt, pen, s_a, s_b, f_a, f_b, pos, steps = refs
    list_positions(plan_ref, col, pos)
    if col == 0:
        plain, count = list_steps(plan_ref, col, steps)
    else:
        steps, plain, count = Part(lists, LISTED_AT), lists[COUNT_AT + 1], lists[COUNT_AT + 2]
    if col == 0:
        load_rows(rows_in, qs)
        for rh in range(QB):
            qt[rh] = qs[rh].astype(f32).T.astype(bf16)
    sort_keys(plan_ref, col, kv_ref, ks, vs, pen)
    turn(vs, vt)
    o_ref[...] = jnp.zeros_like(o_ref)
    for rh in range(QB):
        st_ref[rh, 0:1, :] = jnp.full((1, ROWS), LOWEST, f32)
        st_ref[rh, 1:2, :] = jnp.zeros((1, ROWS), f32)
    exps[0] = jnp.zeros_like(exps[0])
    f_b[...] = jnp.ones_like(f_b)

    def score(t, s_ref):
        _, rh, _, at = step_of(steps, t)
        s_ref[...] = dot(ks[at, :], qt[rh], NN)

    def soften(t, s_ref, f_ref, masked):
        v, rh, c, _ = step_of(steps, t)
        limits = thresholds(plan_ref, pos, v, rh, c)
        offset = offsets()
        for lanes in TILES:
            parts = []
            for i, (seen, late) in enumerate(limits):
                s = s_ref[i * HALF : (i + 1) * HALF, lanes] * SCALE
                penalty = pen[block_rows(c, i), :]
                if masked:
                    s = s - jnp.where(offset >= late, penalty, 0.0)
                    parts.append(jnp.where(offset >= seen, s, LOWEST))
                else:
                    parts.append(s - penalty)
            peak = st_ref[rh, 0:1, lanes]
            tops = functools.reduce(jnp.maximum, parts)
            new_peak = jnp.maximum(peak, jnp.max(tops, axis=0, keepdims=True))
            factor = jnp.exp(peak - new_peak)
            parts = [jnp.exp(s - new_peak) for s in parts]
            total = jnp.sum(sum(parts), axis=0, keepdims=True)
            for i, p in enumerate(parts):
                exps[t, i * HALF : (i + 1) * HALF, lanes] = p.astype(bf16)
            f_ref[0:1, lanes] = factor
            peaks[t, 0:1, lanes] = new_peak
            st_ref[rh, 0:1, lanes] = new_peak
            st_ref[rh, 1:2, lanes] = st_ref[rh, 1:2, lanes] * factor + total

    def attend(t, f_ref):
        _, rh, c, _ = step_of(steps, t)
        o_ref[rh] = o_ref[rh] * f_ref[0:1, :] + dot(turned_piece(vt, c), exps[t], NN)

    score(0, s_a)

    def pair(masked, i, _):
        t = 2 * i
        attend(jnp.maximum(t - 1, 0), f_b)
        score(t + 1, s_b)
        soften(t, s_a, f_a, masked)
        attend(t, f_a)
        score(t + 2, s_a)
        soften(t + 1, s_b, f_b, masked)
        return 0

    pairs = (count + 1) // 2
    lax.fori_loop(0, plain // 2, functools.partial(pair, False), 0)
    lax.fori_loop(plain // 2, pairs, functools.partial(pair, True), 0)
    attend(2 * pairs - 1, f_b)


def weigh_kernel(o0, st0, o1, st1, c0, c1, c2, c3, out_ref, cs, ct):
    for r, ref in enumerate((c0, c1, c2, c3)):
        for half in range(2):
            rh = 2 * r + half
            rows = ref[:, half * HALF : (half + 1) * HALF, :].reshape(ROWS, HD)
            cot = rows.astype(f32).T
            cs[rh] = rows
            ct[rh] = cot.astype(bf16)
            peak = jnp.maximum(st0[rh, 0:1, :], st1[rh, 0:1, :])
            f0, f1 = (jnp.exp(st[rh, 0:1, :] - peak) for st in (st0, st1))
            total = st0[rh, 1:2, :] * f0 + st1[rh, 1:2, :] * f1
            seen = total > 0.0
            weighted = jnp.sum(cot * (o0[rh] * f0 + o1[rh] * f1), axis=0, keepdims=True)
            safe = jnp.where(seen, total, 1.0)
            out_ref[rh : rh + 1, :] = jnp.where(seen, peak + jnp.log(safe), LOWEST)
            out_ref[QB + rh : QB + rh + 1, :] = weighted / safe


def combine(parts):
    peak = functools.reduce(jnp.maximum, [norm for norm, _ in parts])
    shares = [jnp.exp(norm - peak) for norm, _ in parts]
    total = sum(shares)
    return peak + jnp.log(total), sum(share * mean for share, (_, mean) in zip(shares, parts)) / total


def row_pair(ref, n):
    return ref[n : n + 1, :], ref[QB + n : QB + n + 1, :]


def merge_stats(pieces, stats):
    for rh in range(QB):
        norm, mean = combine([row_pair(ref, (rh - 2 * t) % QB) for t, ref in enumerate(pieces)])
        stats[rh, 0:1, :] = norm
        stats[rh, 1:2, :] = mean


def backward_kernel(col, plan_ref, steps, *refs):
    (qs, cs, ct, kv_ref, peaks, exps), pieces, refs = refs[:6], refs[6:10], refs[10:]
    if col == 1:
        dq, dkv_ref, refs = refs[:2], refs[2], refs[3:]
    else:
        dq_before, dq_out, dkv_ref, dq, refs = refs[:2], refs[2:6], refs[6], refs[7:9], refs[9:]
        (turned, sems), refs = refs[:2], refs[2:]
    (ks, vs, kt, stats), dk, dv, dl, refs = refs[:4], refs[4:6], refs[6:8], refs[8:10], refs[10:]
    p_even, p_odd, d_even, d_odd, refs = refs[:2], refs[2:4], refs[4:6], refs[6:8], refs[8:]
    (pos,) = refs
    list_positions(plan_ref, col, pos)
    kept_at, count = Part(steps, KEPT_AT), steps[COUNT_AT]
    sort_keys(plan_ref, col, kv_ref, ks, vs)
    turn(ks, kt)
    for ref in dk + dv + dl + p_odd + d_odd:
        ref[...] = jnp.zeros_like(ref)
    for n in STREAMS:
        dq[n][...] = jnp.zeros_like(dq[n]) if col == 1 else dq_before[n][...]
    merge_stats(pieces, stats)

    def differ(n, t, p_refs, d_refs):
        v, rh, c, _ = stream_step(steps, n, t)
        offset = offsets()
        limits = thresholds(plan_ref, pos, v, rh, c)
        kept = kept_at[v % SKIP]
        shares = [jnp.exp(peaks[kept, 0:1, lanes] - stats[rh, 0:1, lanes]) for lanes in TILES]
        shares = [jnp.where(v >= SKIP, 0.0, share) for share in shares]
        for first in range(0, STEP, 2):
            blocks = (first, first + 1)
            late_sums = [dl[n][block_rows(c, i), :] for i in blocks]
            at = pl.ds(pl.multiple_of(c * CK + first * HALF, SHARD), 2 * HALF)
            for wide in WIDE_TILES:
                grad = dot(vs[at, :], ct[rh, :, wide], NN)
                for m, i in enumerate(blocks):
                    rows = slice(i * HALF, (i + 1) * HALF)
                    for j in range(WIDE // SHARD):
                        here = slice(j * SHARD, (j + 1) * SHARD)
                        lanes = slice(wide.start + here.start, wide.start + here.stop)
                        p = exps[kept, rows, lanes].astype(f32) * shares[lanes.start // SHARD]
                        d = p * (grad[m * HALF : (m + 1) * HALF, here] - stats[rh, 1:2, lanes])
                        late_sums[m] = late_sums[m] + jnp.where(offset >= limits[i][1], d, 0.0)
                        p_refs[n][rows, lanes] = p.astype(bf16)
                        d_refs[n][rows, lanes] = d.astype(bf16)
            for m, i in enumerate(blocks):
                dl[n][block_rows(c, i), :] = late_sums[m]

    def gather(n, t, p_refs, d_refs):
        _, rh, c, at = stream_step(steps, n, t)
        dk[n][at, :] += dot(d_refs[n][...], qs[rh], NN)
        dv[n][at, :] += dot(p_refs[n][...], cs[rh], NN)
        dq[n][rh - n * QS] += dot(turned_piece(kt, c), d_refs[n][...], NN)

    def both(work, *args):
        for n in STREAMS:
            work(n, *args)

    def pair(i, _):
        t = 2 * i
        both(gather, jnp.maximum(t - 1, 0), p_odd, d_odd)
        both(differ, t, p_even, d_even)
        both(gather, t, p_even, d_even)
        both(differ, t + 1, p_odd, d_odd)
        return 0

    lax.fori_loop(0, count // 2, pair, 0)
    both(gather, count - 1, p_odd, d_odd)
    copies = []
    if col == 0:
        for r, ref in enumerate(dq_out):
            for half in range(2):
                rows = (dq[r // 2][2 * (r % 2) + half].T * SCALE).astype(bf16)
                turned[r, :, half * HALF : (half + 1) * HALF, :] = rows.reshape(HEADS, HALF, HD)
            copies.append(pltpu.make_async_copy(turned.at[r], ref, sems.at[r]))
            copies[-1].start()
    for j in range(NZ):
        low = plan_ref[j, SLOT_AT + col]
        spots = [pl.ds(pl.multiple_of(slot * HALF, HALF), HALF) for slot in (low, SLOTS - 1 - low)]
        for half, at in enumerate(spots):
            key_sum = (dk[0][at, :] + dk[1][at, :]) * SCALE
            value_sum = dv[0][at, :] + dv[1][at, :]
            dkv_ref[j, half * HALF : (half + 1) * HALF, :] = key_sum.astype(dkv_ref.dtype)
            dkv_ref[j, SHARD + half * HALF : SHARD + (half + 1) * HALF, :] = value_sum.astype(dkv_ref.dtype)
        late = jnp.concatenate([dl[0][at, :] + dl[1][at, :] for at in spots], axis=0)
        total = jnp.sum(late.T, axis=0, keepdims=True)
        dkv_ref[j, 2 * SHARD : 2 * SHARD + 16, :] = jnp.concatenate(
            [total, jnp.zeros((15, SHARD), f32)], axis=0
        ).astype(dkv_ref.dtype)
    for copy in copies:
        copy.wait()


def total_kernel(parts_ref, logit_ref, dk_ref, dv_ref, dl_ref):
    total = parts_ref[0].astype(f32)
    for n in range(1, NZ):
        total = total + parts_ref[n].astype(f32)
    dk_ref[0] = total[:SHARD]
    dv_ref[0] = total[SHARD : 2 * SHARD]
    dl_ref[...] = -jax.nn.sigmoid(logit_ref[...]) * total[2 * SHARD : 2 * SHARD + 1]


VMEM = pl.BlockSpec(memory_space=pltpu.VMEM)
SMEM = pl.BlockSpec(memory_space=pltpu.SMEM)
HBM = pl.BlockSpec(memory_space=pltpu.HBM)


def grant(mib):
    return pltpu.CompilerParams(vmem_limit_bytes=mib * 1024 * 1024)


MOST = 5 * NA
KEYS = SLOTS * HALF
shaped = jax.ShapeDtypeStruct


def cost(us):
    return pl.CostEstimate(flops=int(us * 1e9), bytes_accessed=2**20, transcendentals=0)


def run_plan(where, block_order):
    return pl.pallas_call(
        functools.partial(plan_kernel, where),
        out_shape=shaped((8, SHARD), i32),
        in_specs=[VMEM],
        out_specs=VMEM,
        compiler_params=grant(4),
        cost_estimate=cost(12),
        name="plan",
    )(block_order.T)


def run_pack(keys, values, logits):
    return pl.pallas_call(
        pack_kernel,
        out_shape=shaped((NZ, KV_ROWS, HD), bf16),
        in_specs=[VMEM] * 3,
        out_specs=VMEM,
        compiler_params=grant(4),
        name="pack",
    )(keys, values, logits)


def run_cotangent(where, pieces, w_out):
    return pl.pallas_call(
        functools.partial(cotangent_kernel, where),
        out_shape=shaped((HEADS, SHARD, HD), bf16),
        in_specs=[VMEM] * 5,
        out_specs=VMEM,
        scratch_shapes=[pltpu.VMEM((SHARD, w_out.shape[1]), bf16)],
        compiler_params=grant(8),
        cost_estimate=cost(5),
        name="cotangent",
    )(*pieces, w_out)


def run_forward(col, plan, q, kv, lists=()):
    out_shape = (
        shaped((QB, HD, ROWS), f32),
        shaped((QB, 2, ROWS), f32),
        shaped((MOST, 1, ROWS), f32),
        shaped((MOST, CK, ROWS), bf16),
    )
    if col == 0:
        out_shape += (shaped((QB, ROWS, HD), bf16), shaped((QB, HD, ROWS), bf16))
    o, st, peaks, exps, *turned = pl.pallas_call(
        functools.partial(forward_kernel, col),
        out_shape=out_shape,
        in_specs=[SMEM] + [VMEM] * (len(q) + 1) + [SMEM] * len(lists),
        out_specs=(VMEM,) * len(out_shape),
        scratch_shapes=[
            pltpu.VMEM((KEYS, HD), bf16),
            pltpu.VMEM((KEYS, HD), bf16),
            pltpu.VMEM((KEYS // SHARD, HD, SHARD), bf16),
            pltpu.VMEM((KEYS, SHARD), f32),
            pltpu.VMEM((CK, ROWS), f32),
            pltpu.VMEM((CK, ROWS), f32),
            pltpu.VMEM((8, ROWS), f32),
            pltpu.VMEM((8, ROWS), f32),
            pltpu.SMEM((SLOTS,), i32),
            pltpu.SMEM((QB * PER_BLOCK + 3,), i32),
        ],
        compiler_params=grant(14),
        cost_estimate=cost(10),
        name=f"forward{col}",
    )(plan, *q, kv, *lists)
    return (o, st), (peaks, exps), turned


def run_weigh(sums, cot):
    return pl.pallas_call(
        weigh_kernel,
        out_shape=(
            shaped((2 * QB, ROWS), f32),
            shaped((QB, ROWS, HD), bf16),
            shaped((QB, HD, ROWS), bf16),
        ),
        in_specs=[VMEM] * 8,
        out_specs=(VMEM,) * 3,
        compiler_params=grant(8),
        name="weigh",
    )(*sums, *cot)


def run_backward(col, plan, lists, rows, kv, exps, stats, dq_sum=()):
    sums = [pltpu.VMEM((QS, HD, ROWS), f32)] * 2
    if col == 1:
        scratch = []
        out_shape = (shaped((QS, HD, ROWS), f32),) * 2 + (shaped((NZ, KV_ROWS, HD), bf16),)
        out_specs = (VMEM,) * 3
    else:
        scratch = sums + [
            pltpu.VMEM((NA, HEADS, SHARD, HD), bf16),
            pltpu.SemaphoreType.DMA((NA,)),
        ]
        out_shape = (shaped((HEADS, SHARD, HD), bf16),) * NA + (shaped((NZ, KV_ROWS, HD), f32),)
        out_specs = (HBM,) * NA + (VMEM,)
    return pl.pallas_call(
        functools.partial(backward_kernel, col),
        out_shape=out_shape,
        in_specs=[SMEM] * 2 + [VMEM] * (10 + len(dq_sum)),
        out_specs=out_specs,
        scratch_shapes=scratch
        + [
            pltpu.VMEM((KEYS, HD), bf16),
            pltpu.VMEM((KEYS, HD), bf16),
            pltpu.VMEM((KEYS // SHARD, HD, SHARD), bf16),
            pltpu.VMEM((QB, 2, ROWS), f32),
        ]
        + [pltpu.VMEM((KEYS, HD), f32)] * 6
        + [pltpu.VMEM((CK, ROWS), bf16)] * 8
        + [pltpu.SMEM((SLOTS,), i32)],
        compiler_params=grant(22),
        cost_estimate=cost(15),
        name=f"backward{col}",
    )(plan, lists, *rows, kv, *exps, *stats, *dq_sum)


def run_lists(plan):
    return pl.pallas_call(
        lists_kernel,
        out_shape=(shaped((LISTS,), i32),) * 2,
        in_specs=[SMEM],
        out_specs=(SMEM,) * 2,
        compiler_params=grant(4),
        cost_estimate=cost(2),
        name="lists",
    )(plan)


def run_total(parts, logits):
    return pl.pallas_call(
        total_kernel,
        out_shape=(shaped((1, SHARD, HD), f32), shaped((1, SHARD, HD), f32), shaped((1, SHARD), f32)),
        in_specs=[VMEM] * 2,
        out_specs=(VMEM,) * 3,
        compiler_params=grant(4),
        name="total",
    )(parts, logits)


def from_y(x, r):
    return lax.ppermute(x, "y", [((i + r) % NA, i) for i in range(NA)])


def gather_y(x):
    return [x] + [from_y(x, r) for r in range(1, NA)]


def swap(x, axis):
    return lax.ppermute(x, axis, [(0, 1), (1, 0)])


def place():
    return lax.axis_index("y"), lax.axis_index("z"), lax.axis_index("xl")


def head_place():
    return lax.axis_index("xh"), lax.axis_index("core")


def per_device(queries, keys, values, evict_logits, block_order, grad_y, w_out):
    plan = run_plan(place, block_order)
    keys, plan = lax.optimization_barrier((keys, plan))
    kv = lax.all_to_all(run_pack(keys, values, evict_logits), "z", 0, 0, tiled=True)
    over = swap(grad_y, "xh")
    pieces = (grad_y, over, swap(grad_y, "core"), swap(over, "core"))
    q_all = gather_y(queries)
    cot = run_cotangent(head_place, pieces, w_out)
    kv_other = swap(kv, "xl")
    cot_all = gather_y(cot)
    sums0, exps0, (qs, qt) = run_forward(0, plan, q_all, kv)
    qt, plan = lax.optimization_barrier((qt, plan))
    lists0, lists1 = run_lists(plan)
    sums1, exps1, _ = run_forward(1, plan, (qt,), kv_other, (lists1,))
    stats, cs, ct = run_weigh((*sums0, *sums1), cot_all)
    rows = (qs, cs, ct)
    stats = gather_y(stats)
    *dq_sum, dkv_other = run_backward(1, plan, lists1, rows, kv_other, exps1, stats)
    dkv_here = swap(dkv_other, "xl")
    *dq, dkv = run_backward(0, plan, lists0, rows, kv, exps0, stats, dq_sum)
    dkv = (dkv + dkv_here.astype(f32)).astype(bf16)
    dkv = lax.all_to_all(dkv, "z", 0, 0, tiled=True)
    key_grad, value_grad, logit_grad = run_total(dkv, evict_logits)
    query_grad = dq[0].astype(f32)
    for r in (2, 1, 3):
        query_grad = query_grad + from_y(dq[r], NA - r).astype(f32)
    return query_grad.astype(bf16), key_grad, value_grad, logit_grad


def solution(mesh):
    split = Mesh(mesh.devices.reshape(4, 8, 2, 2, 2), ("y", "z", "xl", "xh", "core"))
    ctx, head = ("y", "z", "xl"), ("xh", "core")
    return jax.shard_map(
        per_device,
        mesh=split,
        in_specs=(
            P(head, ctx, None),
            P(head, ctx, None),
            P(head, ctx, None),
            P(head, ctx),
            P(),
            P(ctx + head, None),
            P(head, None),
        ),
        out_specs=(
            P(head, ctx, None),
            P(head, ctx, None),
            P(head, ctx, None),
            P(head, ctx),
        ),
        check_vma=False,
    )
```
